32 devices in a mesh: rep: 8 (over z, y), fsdp: 4 (over x, core).
Axes of the slice: x: 2, y: 2, z: 4, core: 2. Of those that a mesh axis runs over, the one named last changes fastest.
Arguments:
- hidden: bfloat16 [8, 1024, 4096], P('rep', 'fsdp'), may hold values from -6 to 6
- key_grad: bfloat16 [8, 1024, 512], P('rep', 'fsdp'), may hold values from -0.1875 to 0.1875
- weight: float32 [8, 4096, 512], P('rep', 'fsdp'), may hold values from -0.09375 to 0.09375
- moment1: bfloat16 [8, 4096, 512], P('rep', 'fsdp'), may hold values from -3 to 3
- moment2: bfloat16 [8, 4096, 512], P('rep', 'fsdp'), may hold values from 0.19921875 to 2
- step: int32 [], replicated, may hold values from 0 to 999
Outputs:
- keys: bfloat16 [8, 1024, 512], P('rep', 'fsdp')
- input_grad: bfloat16 [8, 1024, 4096], P('rep', 'fsdp')
- weight_next: float32 [8, 4096, 512], P('rep', 'fsdp')
- moment1_next: bfloat16 [8, 4096, 512], P('rep', 'fsdp')
- moment2_next: bfloat16 [8, 4096, 512], P('rep', 'fsdp')
The draws below stay inside these ranges and needn't reach their ends.
All inputs are finite; a program needn't handle non-finite values.
Results may differ from the reference program's by a relative error of at most 0.005.
Values may be sent and summed in bfloat16 or wider, within the bound.
No kernel may reach another device: no remote copies, remote signals or barrier semaphores. Data moves between devices by JAX's collectives and lax.ppermute only.
A program may use at most 64 MiB of HBM per device.

```python
import math
import jax
import jax.numpy as jnp
from jax import lax

D = 4096
KV = 512
TOK_REP = 1024
LEVELS = 6
N_REP = 8


def with_spikes(drawn, rng, source, target, parts, factor):
    owner, partner = [(jnp.arange(drawn.shape[axis_at]) // (drawn.shape[axis_at] // parts)).reshape([-1 if axis == axis_at else 1 for axis in range(drawn.ndim)]) for axis_at in (source, target)]
    chosen = jax.random.permutation(rng, parts)[partner]
    strong = (owner == chosen) | (owner == (partner + parts // 2) % parts)
    return jnp.where(strong, factor * drawn, drawn)


def level_of(rng, extent, pieces, smallest, top_value):
    loudness, own = 1.0, jax.random.fold_in(rng, 6)
    for axis_at, parts in pieces:
        heights = jnp.exp(jax.random.uniform(jax.random.fold_in(own, axis_at), (parts,), jnp.float32, smallest / len(pieces), top_value / len(pieces)))
        loudness = loudness * jnp.repeat(heights, extent[axis_at] // parts).reshape([-1 if axis == axis_at else 1 for axis in range(len(extent))])
    return loudness


def noise(rng, shape, spread, reach, shards=(), dtype=jnp.bfloat16):
    values = spread * jax.random.normal(rng, shape, jnp.float32)
    if shards:
        values = values * level_of(rng, shape, shards, -0.22, 0.18)
    return jnp.clip(values, -reach, reach).astype(dtype)


def gaussian_with(own_key, dims, deviation, bound, pieces, heavy, held_as=jnp.bfloat16):
    entries = deviation * jax.random.normal(own_key, dims, jnp.float32)
    if pieces:
        entries = entries * level_of(own_key, dims, pieces, -0.22, 0.18)
    return jnp.clip(with_spikes(entries, jax.random.fold_in(own_key, 3), *heavy), -bound, bound).astype(held_as)


def setup_inputs(seed: int = 0) -> dict:
    streams_of = jax.random.split(jax.random.key(seed), 7)
    return {
        "hidden": gaussian_with(streams_of[0], (N_REP, TOK_REP, D), 1.0, 6.0, ((0, 8), (1, 4)), (1, 2, 4, 2.0)),
        "key_grad": noise(streams_of[1], (N_REP, TOK_REP, KV), TOK_REP ** -0.5, 0.1875, ((0, 8), (1, 4))),
        "weight": noise(streams_of[2], (N_REP, D, KV), D ** -0.5, 0.09375, ((0, 8), (1, 4)), jnp.float32),
        "moment1": noise(streams_of[3], (N_REP, D, KV), 0.3, 3.0, ((0, 8), (1, 4))),
        "moment2": jnp.clip(jnp.exp(math.log(2.0) - 2.306499 * jax.random.uniform(streams_of[4], (N_REP, D, KV), jnp.float32) ** level_of(streams_of[4], (N_REP, D, KV), ((0, 8), (1, 4)), -0.2, 0.2)), 0.19921875, 2.0).astype(jnp.bfloat16),
        "step": jax.random.randint(streams_of[5], (), 0, 1000).astype(jnp.int32),
    }


def replica_pass(operands):
    tokens_in, cotangent, weight_half = operands
    keys_full = jnp.dot(tokens_in, weight_half, preferred_element_type=jnp.float32)
    back_full = lax.dot_general(cotangent, weight_half, (((1,), (1,)), ((), ())), preferred_element_type=jnp.float32)
    grad_full = lax.dot_general(tokens_in, cotangent, (((0,), (0,)), ((), ())), preferred_element_type=jnp.float32)
    return (keys_full.astype(jnp.bfloat16), back_full.astype(jnp.bfloat16), grad_full)

def reference(hidden, key_grad, weight, moment1, moment2, step):
    weight_half = weight.astype(jnp.bfloat16)
    keys, input_grad, grad = lax.map(replica_pass, (hidden, key_grad, weight_half))
    count = (step + 1).astype(jnp.float32)
    first = 0.9 * moment1.astype(jnp.float32) + 0.1 * grad
    second = 0.95 * moment2.astype(jnp.float32) + 0.05 * grad * grad
    first_hat = first / (1.0 - jnp.power(jnp.float32(0.9), count))
    second_hat = second / (1.0 - jnp.power(jnp.float32(0.95), count))
    updated = weight - 0.003 * (first_hat / (jnp.sqrt(second_hat) + 1e-08) + 0.1 * weight)
    distance = jnp.left_shift(jnp.int32(1), (step % LEVELS).astype(jnp.int32)) % N_REP
    neighbour = jnp.roll(updated, distance, axis=0)
    weight_next = 0.5 * (updated + neighbour)
    return (keys, input_grad, weight_next, first.astype(jnp.bfloat16), second.astype(jnp.bfloat16))
```

```python
import functools

import jax
import jax.numpy as jnp
from jax import lax
from jax.experimental import pallas as pl
from jax.experimental.pallas import tpu as pltpu
from jax.sharding import PartitionSpec as P

LEVELS = 6
CORES = 2
PAD = 16
STRIP = 128
F32 = jnp.float32
BF16 = jnp.bfloat16
ANY = pl.BlockSpec(memory_space=pl.ANY)
HBM = pl.BlockSpec(memory_space=pltpu.HBM)
SMEM = pl.BlockSpec(memory_space=pltpu.SMEM)
VMEM = pl.BlockSpec(memory_space=pltpu.VMEM)
PARAMS = pltpu.CompilerParams(vmem_limit_bytes=16 * 2**20)
OVER_ROWS = (((0,), (0,)), ((), ()))
OVER_COLUMNS = (((1,), (1,)), ((), ()))


def call(kernel, name, **kwargs):
    with jax.named_scope("at_" + name):
        return pl.pallas_call(kernel, name=name, compiler_params=PARAMS, **kwargs)


def like(shape, dtype):
    return jax.ShapeDtypeStruct(shape, dtype)


def core_swap(value, name):
    n = lax.axis_size("fsdp")
    with jax.named_scope("at_" + name):
        return lax.ppermute(value, "fsdp", [(i, i ^ 1) for i in range(n)])


def chip_shift(value, distance, name):
    n = lax.axis_size("fsdp")
    with jax.named_scope("at_" + name):
        return lax.ppermute(value, "fsdp", [(i, (i + CORES * distance) % n) for i in range(n)])


def rep_shift(value, distance, name):
    n = lax.axis_size("rep")
    with jax.named_scope("at_" + name):
        return lax.ppermute(value, "rep", [((i - distance) % n, i) for i in range(n)])


def after(value, *done):
    return lax.optimization_barrier((value, *done))[0]


def shard_at(chip_step, other_core):
    n = lax.axis_size("fsdp")
    me = lax.axis_index("fsdp")
    core = lax.rem(me, CORES)
    if other_core:
        core = 1 - core
    return lax.rem(lax.div(me, CORES) + n // CORES - chip_step, n // CORES) * CORES + core


def cast_rows(weight, spans):
    kv = weight.shape[1]
    total = sum(spans[-1])

    def kernel(src, *outs):
        for (first, size), out in zip(spans, outs):
            out[...] = src[first : first + size, :].astype(BF16)

    return call(
        kernel,
        "cast",
        grid=(1,),
        in_specs=[pl.BlockSpec((total, kv), lambda g: (0, 0))],
        out_specs=[pl.BlockSpec((size, kv), lambda g: (0, 0)) for _, size in spans],
        out_shape=[like((size, kv), BF16) for _, size in spans],
    )(weight)


def partial_grad(own, sib, cot, cot_sib, chip_step, spans, dtype, deps):
    kv = cot.shape[1]
    tokens = own.shape[0]
    rows = own.shape[1] // lax.axis_size("fsdp")

    def kernel(*refs):
        mine, theirs, cot_ref, cot_sib_ref = refs[:4]
        for (first, size, pad), out in zip(spans, refs[4 + len(deps) :]):
            at = slice(first, first + size)
            total = lax.dot_general(mine[:, at], cot_ref[...], OVER_ROWS, preferred_element_type=F32)
            total += lax.dot_general(theirs[:, at], cot_sib_ref[...], OVER_ROWS, preferred_element_type=F32)
            out[:size, :] = total.astype(dtype)
            if pad:
                out[size:, :] = jnp.zeros((pad, kv), dtype)

    columns = pl.BlockSpec((tokens, rows), lambda g: (0, shard_at(chip_step, False)))
    whole = pl.BlockSpec((tokens, kv), lambda g: (0, 0))
    return call(
        kernel,
        "partial",
        grid=(1,),
        in_specs=[columns, columns, whole, whole] + [ANY] * len(deps),
        out_specs=[pl.BlockSpec((size + pad, kv), lambda g: (0, 0)) for _, size, pad in spans],
        out_shape=[like((size + pad, kv), dtype) for _, size, pad in spans],
    )(own, sib, cot, cot_sib, *deps)


def adam_rows(span, grad, got, weight, moments, fixes, so_far, send, deps):
    first, size, pad = span
    rows, kv = weight.shape
    count = len(got)
    kept = 2 if send else 3

    def kernel(*refs):
        fix1, fix2, grad_ref = refs[:3]
        got_refs = refs[3 : 3 + count]
        w_ref, m_ref, v_ref = refs[3 + count : 6 + count]
        at = 6 + count + (kept if so_far else 0) + len(deps)
        places = refs[at : at + kept]
        at += kept
        if send:
            up_out, short_out = refs[at : at + 2]
            at += 2
        bufs, sems = refs[at : at + kept], refs[at + kept]
        copies = []
        for strip in range(0, size, STRIP):
            here = slice(strip, strip + STRIP)
            there = slice(first + strip, first + strip + STRIP)
            g = grad_ref[there, :]
            for ref in got_refs:
                g += ref[here, :].astype(F32)
            w = w_ref[there, :]
            m = 0.9 * m_ref[there, :].astype(F32) + 0.1 * g
            v = 0.95 * v_ref[there, :].astype(F32) + 0.05 * g * g
            up = w - 0.003 * ((m / fix1[0]) / (jnp.sqrt(v / fix2[0]) + 1e-8) + 0.1 * w)
            bufs[0][here, :] = m.astype(BF16)
            bufs[1][here, :] = v.astype(BF16)
            if send:
                up_out[here, :] = up
                short_out[here, :] = up.astype(BF16)
            else:
                bufs[2][here, :] = up
            for j in range(kept):
                copies.append(
                    pltpu.make_async_copy(
                        bufs[j].at[pl.ds(strip, STRIP), :],
                        places[j].at[0, pl.ds(first + strip, STRIP), :],
                        sems.at[j, strip // STRIP],
                    )
                )
                copies[-1].start()
        if send and pad:
            short_out[size:, :] = jnp.zeros((pad, kv), BF16)
        for copy in copies:
            copy.wait()

    kinds = [BF16, BF16] + ([] if send else [F32])
    return call(
        kernel,
        "adam",
        in_specs=[SMEM, SMEM] + [VMEM] * (4 + count) + [HBM] * (kept if so_far else 0) + [ANY] * len(deps),
        out_specs=[HBM] * kept + ([VMEM, VMEM] if send else []),
        out_shape=[pltpu.HBM((1, rows, kv), kind) for kind in kinds]
        + ([like((size, kv), F32), like((size + pad, kv), BF16)] if send else []),
        scratch_shapes=[pltpu.VMEM((size, kv), kind) for kind in kinds]
        + [pltpu.SemaphoreType.DMA((kept, size // STRIP))],
        input_output_aliases={6 + count + i: i for i in range(kept)} if so_far else {},
    )(*fixes, grad, *got, weight, *moments, *(so_far or ()), *deps)


def project(pieces, own, cot, so_far, last, deps, emit=()):
    tokens, width = own.shape
    kv = cot.shape[1]
    shard = width // lax.axis_size("fsdp")
    count = len(pieces)
    sizes = [piece[1] for piece in pieces]

    def kernel(*refs):
        weights, (cot_ref, own_ref) = refs[:count], refs[count : count + 2]
        at = count + 2
        if so_far:
            keys_ref = refs[at]
            at += 2
        at += len(deps)
        keys_out, back_out = refs[at : at + 2]
        spans_out = refs[at + 2 : at + 2 + len(emit)]
        at += 2 + len(emit)
        cols, outs = refs[at : at + count], refs[at + count : at + 2 * count]
        keys_buf, sems = refs[-2:]
        loads, stores = [], []
        for j, (_, _, steps, other, first) in enumerate(pieces):
            place = pl.ds(pl.multiple_of(shard_at(steps, other) * shard + first, 128), sizes[j])
            loads.append(pltpu.make_async_copy(own_ref.at[:, place], cols[j], sems.at[0, j]))
            stores.append(pltpu.make_async_copy(outs[j], back_out.at[0, :, place], sems.at[1, j]))
            loads[j].start()
        for (first, size), out in zip(emit, spans_out):
            out[...] = weights[0][first : first + size, :].astype(BF16)
        for j in range(count):
            outs[j][...] = lax.dot_general(
                cot_ref[...], weights[j][: sizes[j], :].astype(BF16), OVER_COLUMNS, preferred_element_type=F32
            ).astype(BF16)
            stores[j].start()
        total = None
        for j in range(count):
            loads[j].wait()
            term = jnp.dot(cols[j][...], weights[j][: sizes[j], :].astype(BF16), preferred_element_type=F32)
            total = term if total is None else total + term
        if so_far:
            total += keys_ref[...]
        if last:
            keys_buf[...] = total.astype(BF16)
            store = pltpu.make_async_copy(keys_buf, keys_out.at[0], sems.at[0, count])
            store.start()
            store.wait()
        else:
            keys_out[...] = total
        for j in range(count):
            stores[j].wait()

    return call(
        kernel,
        "project",
        in_specs=[VMEM] * (count + 1) + [ANY] + ([VMEM, HBM] if so_far else []) + [ANY] * len(deps),
        out_specs=[HBM if last else VMEM, HBM] + [VMEM] * len(emit),
        out_shape=[
            pltpu.HBM((1, tokens, kv), BF16) if last else like((tokens, kv), F32),
            pltpu.HBM((1, tokens, width), BF16),
        ]
        + [like((size, kv), BF16) for _, size in emit],
        scratch_shapes=[pltpu.VMEM((tokens, size), BF16) for size in sizes] * 2
        + [pltpu.VMEM((tokens, kv), BF16), pltpu.SemaphoreType.DMA((2, count + 1))],
        input_output_aliases={count + 3: 1} if so_far else {},
    )(*[piece[0] for piece in pieces], cot, own, *(so_far or ()), *deps)


def average(spans, updated, neighbours, deps):
    rows, kv = sum(size for _, size, _ in spans), updated[0].shape[1]
    count = len(spans)

    def kernel(*refs):
        out, buf, sems = refs[-3:]
        copies = []
        for j, (first, size, _) in enumerate(spans):
            for strip in range(0, size, STRIP):
                here = slice(strip, strip + STRIP)
                at = first + strip
                buf[at : at + STRIP, :] = 0.5 * (refs[j][here, :] + refs[count + j][here, :].astype(F32))
                copies.append(
                    pltpu.make_async_copy(
                        buf.at[pl.ds(at, STRIP), :], out.at[0, pl.ds(at, STRIP), :], sems.at[at // STRIP]
                    )
                )
                copies[-1].start()
        for copy in copies:
            copy.wait()

    return call(
        kernel,
        "average",
        in_specs=[VMEM] * (2 * count) + [ANY] * len(deps),
        out_specs=HBM,
        out_shape=pltpu.HBM((1, rows, kv), F32),
        scratch_shapes=[pltpu.VMEM((rows, kv), F32), pltpu.SemaphoreType.DMA((rows // STRIP,))],
    )(*updated, *neighbours, *deps)


def make_branch(distance):
    def branch(hidden, key_grad, weight, moment1, moment2, step):
        chips = lax.axis_size("fsdp") // CORES
        own, cot, w = hidden[0], key_grad[0], weight[0]
        moments = (moment1[0], moment2[0])
        rows = w.shape[0]
        half, eighth = rows // 2, rows // 8
        count = (step + 1).astype(F32)
        fixes = [(1.0 - jnp.power(F32(b), count)).reshape(1) for b in (0.9, 0.95)]
        far = range(1, chips)

        sib = core_swap(own, "hidden")
        cot_sib = core_swap(cot, "cot")
        w_sib = core_swap(w, "w_sib")
        local = [(w, rows, 0, False, 0), (w_sib, rows, 0, True, 0)]

        def send_far(part, i):
            return [chip_shift(part, s, f"far{i}") for s in far]

        def pieces_of(i, arrays, order):
            first, size = w_spans[i]
            return [(v, size, s, False, first) for v, s in zip(arrays, far)] + [
                (core_swap(after(v, *order), f"swap{i}"), size, s, True, first) for v, s in zip(arrays, far)
            ]

        def adam(i, state, deps):
            return adam_rows(
                g_spans[i], grad, [got[s][i] for s in far], w, moments, fixes, state, bool(distance), deps
            )

        def partial(s, spans, dtype, deps):
            return partial_grad(own, sib, cot, cot_sib, -s % chips, spans, dtype, deps)

        if distance:
            g_spans = [(0, half, PAD), (half, half, 0)]
            w_spans = [(0, 2 * eighth), (2 * eighth, 3 * eighth), (5 * eighth, 3 * eighth)]
            (w0,) = cast_rows(w, [(0, 2 * eighth + PAD)])
            there0 = send_far(w0, 0)
            sent = {s: partial(s, g_spans, BF16, [w0]) for s in far}
            got = {s: [chip_shift(part, s, f"grad{i}") for i, part in enumerate(sent[s])] for s in far}
            keys, back, w1, w2 = project(
                local, own, cot, None, False, [sent[s][-1] for s in far], w_spans[1:]
            )
            there1, there2 = send_far(w1, 1), send_far(w2, 2)
            (grad,) = partial(0, [(0, rows, 0)], F32, [w2])
            pieces = pieces_of(0, there0, [grad])
            keys, back = project(pieces, own, cot, (keys, back), False, [grad])
            *state, up0, short0 = adam(0, None, [keys])
            near0 = rep_shift(short0, distance, "near0")
            *state, up1, short1 = adam(1, state, [short0])
            near1 = rep_shift(short1, distance, "near1")
            pieces = pieces_of(1, there1, [short1])
            pieces += pieces_of(2, there2, [short1])
            keys, back = project(pieces, own, cot, (keys, back), True, [short1])
            updated = average(g_spans, [up0, up1], [near0, near1], [keys])
        else:
            g_spans = [(0, half, 2 * PAD), (half, half, PAD)]
            w_spans = [(0, half), (half, half)]
            w0, w1 = cast_rows(w, w_spans)
            there0, there1 = send_far(w0, 0), send_far(w1, 1)
            sent = {s: partial(s, g_spans, BF16, [w0]) for s in far}
            got = {s: [chip_shift(part, s, f"grad{i}") for i, part in enumerate(sent[s])] for s in far}
            keys, back = project(local, own, cot, None, False, [sent[s][-1] for s in far])
            (grad,) = partial(0, [(0, rows, 0)], F32, [keys])
            pieces = pieces_of(0, there0, [grad]) + pieces_of(1, there1, [grad])
            keys, back = project(pieces, own, cot, (keys, back), True, [grad])
            state = adam(0, None, [keys])
            state = adam(1, state, [])
            updated = state[2]
        return keys, back, updated, state[0], state[1]

    return branch


def per_device(hidden, key_grad, weight, moment1, moment2, step):
    replicas = lax.axis_size("rep")
    distances = [2**level % replicas for level in range(LEVELS)]
    kinds = sorted(set(distances))
    level = lax.rem(step, LEVELS)
    pick = jnp.int32(0)
    for i, d in enumerate(distances):
        pick = jnp.where(level == i, kinds.index(d), pick)
    return lax.switch(
        pick, [make_branch(d) for d in kinds], hidden, key_grad, weight, moment1, moment2, step
    )


def solution(mesh):
    spec = P("rep", "fsdp", None)
    return jax.shard_map(
        per_device,
        mesh=mesh,
        in_specs=(spec,) * 5 + (P(),),
        out_specs=(spec,) * 5,
        check_vma=False,
    )
```

```python
import jax
import jax.numpy as jnp
from jax import lax
from jax.experimental import pallas as pl
from jax.experimental.pallas import tpu as pltpu
from jax.sharding import PartitionSpec as P

LEVELS = 6
CORES = 2
PAD = 16
STRIP = 128
F32 = jnp.float32
BF16 = jnp.bfloat16
ANY = pl.BlockSpec(memory_space=pl.ANY)
HBM = pl.BlockSpec(memory_space=pltpu.HBM)
SMEM = pl.BlockSpec(memory_space=pltpu.SMEM)
VMEM = pl.BlockSpec(memory_space=pltpu.VMEM)
PARAMS = pltpu.CompilerParams(vmem_limit_bytes=16 * 2**20)
OVER_ROWS = (((0,), (0,)), ((), ()))
OVER_COLUMNS = (((1,), (1,)), ((), ()))


def call(kernel, name, **kwargs):
    with jax.named_scope("at_" + name):
        return pl.pallas_call(kernel, name=name, compiler_params=PARAMS, **kwargs)


def like(shape, dtype):
    return jax.ShapeDtypeStruct(shape, dtype)


def core_swap(value, name):
    n = lax.axis_size("fsdp")
    with jax.named_scope("at_" + name):
        return lax.ppermute(value, "fsdp", [(i, i ^ 1) for i in range(n)])


def chip_shift(value, distance, name):
    n = lax.axis_size("fsdp")
    with jax.named_scope("at_" + name):
        return lax.ppermute(value, "fsdp", [(i, (i + CORES * distance) % n) for i in range(n)])


def rep_shift(value, distance, name):
    n = lax.axis_size("rep")
    with jax.named_scope("at_" + name):
        return lax.ppermute(value, "rep", [((i - distance) % n, i) for i in range(n)])


def after(value, *done):
    return lax.optimization_barrier((value, *done))[0]


def shard_at(chip_step, other_core):
    n = lax.axis_size("fsdp")
    me = lax.axis_index("fsdp")
    core = lax.rem(me, CORES)
    if other_core:
        core = 1 - core
    return lax.rem(lax.div(me, CORES) + n // CORES - chip_step, n // CORES) * CORES + core


def spans_of(rows, shares, pads=None):
    unit = rows // sum(shares)
    pads = pads or (0,) * len(shares)
    return [(sum(shares[:i]) * unit, share * unit, pads[i]) for i, share in enumerate(shares)]


def strips_of(size):
    return [(at, min(STRIP, size - at)) for at in range(0, size, STRIP)]


def cast_rows(weight, spans, deps):
    kv = weight.shape[1]
    low, high = spans[0][0], sum(spans[-1])

    def kernel(src, *refs):
        buf, sem = refs[-2:]
        load = pltpu.make_async_copy(src.at[pl.ds(low, high - low), :], buf, sem)
        load.start()
        load.wait()
        for (first, size), out in zip(spans, refs[len(deps) :]):
            out[...] = buf[first - low : first - low + size, :].astype(BF16)

    return call(
        kernel,
        "cast",
        in_specs=[ANY] * (1 + len(deps)),
        out_specs=[VMEM] * len(spans),
        out_shape=[like((size, kv), BF16) for _, size in spans],
        scratch_shapes=[pltpu.VMEM((high - low, kv), F32), pltpu.SemaphoreType.DMA],
    )(weight, *deps)


def partial_grad(own, sib, cot, cot_sib, chip_step, spans, dtype, deps):
    kv = cot.shape[1]
    tokens = own.shape[0]
    rows = own.shape[1] // lax.axis_size("fsdp")

    def kernel(*refs):
        mine, theirs, cot_ref, cot_sib_ref = refs[:4]
        total = lax.dot_general(mine[...], cot_ref[...], OVER_ROWS, preferred_element_type=F32)
        total += lax.dot_general(theirs[...], cot_sib_ref[...], OVER_ROWS, preferred_element_type=F32)
        for (first, size, pad), out in zip(spans, refs[4 + len(deps) :]):
            out[:size, :] = total[first : first + size, :].astype(dtype)
            if pad:
                out[size:, :] = jnp.zeros((pad, kv), dtype)

    columns = pl.BlockSpec((tokens, rows), lambda g: (0, shard_at(chip_step, False)))
    whole = pl.BlockSpec((tokens, kv), lambda g: (0, 0))
    return call(
        kernel,
        "partial",
        grid=(1,),
        in_specs=[columns, columns, whole, whole] + [ANY] * len(deps),
        out_specs=[pl.BlockSpec((size + pad, kv), lambda g: (0, 0)) for _, size, pad in spans],
        out_shape=[like((size + pad, kv), dtype) for _, size, pad in spans],
    )(own, sib, cot, cot_sib, *deps)


def adam_rows(span, grad, got, weight, moments, scales, so_far, send, deps):
    first, size, pad = span
    rows, kv = weight.shape
    count = len(got)
    kept = 2 if send else 3
    strips = strips_of(size)

    def kernel(*refs):
        scale1_ref, scale2_ref, grad_ref = refs[:3]
        got_refs = refs[3 : 3 + count]
        w_ref, m_ref, v_ref = refs[3 + count : 6 + count]
        at = 6 + count + (kept if so_far else 0) + len(deps)
        places = refs[at : at + kept]
        at += kept
        if send:
            up_out, short_out = refs[at : at + 2]
            at += 2
        bufs, sems = refs[at : at + kept], refs[at + kept]
        copies = []
        scale1, scale2 = scale1_ref[0], scale2_ref[0]
        for i, (strip, high) in enumerate(strips):
            here = slice(strip, strip + high)
            there = slice(first + strip, first + strip + high)
            g = grad_ref[there, :]
            for ref in got_refs:
                g += ref[here, :].astype(F32)
            w = w_ref[there, :]
            m = 0.9 * m_ref[there, :].astype(F32) + 0.1 * g
            v = 0.95 * v_ref[there, :].astype(F32) + 0.05 * g * g
            up = w - 0.003 * ((m * scale1) / (jnp.sqrt(v * scale2) + 1e-8) + 0.1 * w)
            bufs[0][here, :] = m.astype(BF16)
            bufs[1][here, :] = v.astype(BF16)
            if send:
                up_out[here, :] = up
                short_out[here, :] = up.astype(BF16)
            else:
                bufs[2][here, :] = up
            for j in range(kept):
                copies.append(
                    pltpu.make_async_copy(
                        bufs[j].at[pl.ds(strip, high), :],
                        places[j].at[0, pl.ds(first + strip, high), :],
                        sems.at[j, i],
                    )
                )
                copies[-1].start()
        if send and pad:
            short_out[size:, :] = jnp.zeros((pad, kv), BF16)
        for copy in copies:
            copy.wait()

    kinds = [BF16, BF16] + ([] if send else [F32])
    return call(
        kernel,
        "adam",
        in_specs=[SMEM, SMEM] + [VMEM] * (4 + count) + [HBM] * (kept if so_far else 0) + [ANY] * len(deps),
        out_specs=[HBM] * kept + ([VMEM, VMEM] if send else []),
        out_shape=[pltpu.HBM((1, rows, kv), kind) for kind in kinds]
        + ([like((size, kv), F32), like((size + pad, kv), BF16)] if send else []),
        scratch_shapes=[pltpu.VMEM((size, kv), kind) for kind in kinds]
        + [pltpu.SemaphoreType.DMA((kept, len(strips)))],
        input_output_aliases={6 + count + i: i for i in range(kept)} if so_far else {},
    )(*scales, grad, *got, weight, *moments, *(so_far or ()), *deps)


def project(pieces, own, cot, so_far, last, deps, emit=()):
    tokens, width = own.shape
    kv = cot.shape[1]
    shard = width // lax.axis_size("fsdp")
    count = len(pieces)
    sizes = [piece[1] for piece in pieces]

    def kernel(*refs):
        weights, (cot_ref, own_ref) = refs[:count], refs[count : count + 2]
        at = count + 2
        if so_far:
            keys_ref = refs[at]
            at += 2
        at += len(deps)
        keys_out, back_out = refs[at : at + 2]
        spans_out = refs[at + 2 : at + 2 + len(emit)]
        at += 2 + len(emit)
        outs, shorts = refs[at : at + count], refs[at + count : at + count + len(emit)]
        keys_buf, sems = refs[-2:]
        stores = []
        for i, ((first, size), out) in enumerate(zip(emit, spans_out)):
            shorts[i][...] = weights[0][first : first + size, :].astype(BF16)
            stores.append(pltpu.make_async_copy(shorts[i], out, sems.at[count + 1 + i]))
            stores[-1].start()
        total = keys_ref[...] if so_far else None
        for j, (_, _, steps, other, first) in enumerate(pieces):
            place = pl.ds(pl.multiple_of(shard_at(steps, other) * shard + first, 128), sizes[j])
            rows = weights[j][: sizes[j], :].astype(BF16)
            outs[j][...] = lax.dot_general(
                cot_ref[...], rows, OVER_COLUMNS, preferred_element_type=F32
            ).astype(BF16)
            stores.append(pltpu.make_async_copy(outs[j], back_out.at[0, :, place], sems.at[j]))
            stores[-1].start()
            term = jnp.dot(own_ref[:, place], rows, preferred_element_type=F32)
            total = term if total is None else total + term
        if last:
            keys_buf[...] = total.astype(BF16)
            stores.append(pltpu.make_async_copy(keys_buf, keys_out.at[0], sems.at[count]))
            stores[-1].start()
        else:
            keys_out[...] = total
        for store in stores:
            store.wait()

    return call(
        kernel,
        "project",
        in_specs=[VMEM] * (count + 2) + ([VMEM, HBM] if so_far else []) + [ANY] * len(deps),
        out_specs=[HBM if last else VMEM, HBM] + [HBM] * len(emit),
        out_shape=[
            pltpu.HBM((1, tokens, kv), BF16) if last else like((tokens, kv), F32),
            pltpu.HBM((1, tokens, width), BF16),
        ]
        + [pltpu.HBM((size, kv), BF16) for _, size in emit],
        scratch_shapes=[pltpu.VMEM((tokens, size), BF16) for size in sizes]
        + [pltpu.VMEM((size, kv), BF16) for _, size in emit]
        + [pltpu.VMEM((tokens, kv), BF16), pltpu.SemaphoreType.DMA((count + 1 + len(emit),))],
        input_output_aliases={count + 3: 1} if so_far else {},
    )(*[piece[0] for piece in pieces], cot, own, *(so_far or ()), *deps)


def average(rows, spans, updated, neighbours, so_far, deps):
    kv = updated[0].shape[1]
    count = len(spans)
    strips = [(j, first, *strip) for j, (first, size, _) in enumerate(spans) for strip in strips_of(size)]

    def kernel(*refs):
        out, buf, sems = refs[-3:]
        copies = []
        for i, (j, first, strip, high) in enumerate(strips):
            here = slice(strip, strip + high)
            at = pl.ds(first - spans[0][0] + strip, high)
            buf[at, :] = 0.5 * (refs[j][here, :] + refs[count + j][here, :].astype(F32))
            copies.append(
                pltpu.make_async_copy(buf.at[at, :], out.at[0, pl.ds(first + strip, high), :], sems.at[i])
            )
            copies[-1].start()
        for copy in copies:
            copy.wait()

    before = [] if so_far is None else [so_far]
    return call(
        kernel,
        "average",
        in_specs=[VMEM] * (2 * count) + [HBM] * len(before) + [ANY] * len(deps),
        out_specs=HBM,
        out_shape=pltpu.HBM((1, rows, kv), F32),
        scratch_shapes=[
            pltpu.VMEM((sum(size for _, size, _ in spans), kv), F32),
            pltpu.SemaphoreType.DMA((len(strips),)),
        ],
        input_output_aliases={2 * count: 0} if before else {},
    )(*updated, *neighbours, *before, *deps)


def make_branch(distance):
    def branch(hidden, key_grad, weight, moment1, moment2, step):
        chips = lax.axis_size("fsdp") // CORES
        own, cot, w = hidden[0], key_grad[0], weight[0]
        moments = (moment1[0], moment2[0])
        rows = w.shape[0]
        count = (step + 1).astype(F32)
        scales = [(1.0 / (1.0 - jnp.power(F32(b), count))).reshape(1) for b in (0.9, 0.95)]
        far = range(1, chips)

        def local_pieces(w_sib):
            return [(w, rows, 0, False, 0), (w_sib, rows, 0, True, 0)]

        def send_far(part, i):
            return [chip_shift(part, s, f"far{i}") for s in far]

        def pieces_of(i, arrays, order):
            first, size = w_spans[i]
            return [(v, size, s, False, first) for v, s in zip(arrays, far)] + [
                (core_swap(after(v, *order), f"swap{i}"), size, s, True, first) for v, s in zip(arrays, far)
            ]

        def adam(i, state, deps):
            return adam_rows(
                g_spans[i], grad, [got[s][i] for s in far], w, moments, scales, state, bool(distance), deps
            )

        def partial(s, spans, dtype, deps):
            return partial_grad(own, sib, cot, cot_sib, -s % chips, spans, dtype, deps)

        if distance:
            heavy = 2 * distance >= lax.axis_size("rep")
            g_spans = spans_of(rows, (28, 36) if heavy else (25, 20, 19))
            w_spans = [span[:2] for span in spans_of(rows, (2, 3, 3))]
            first, size = w_spans[0]
            sib, cot_sib = core_swap(own, "hidden"), core_swap(cot, "cot")
            (w0,) = cast_rows(w, [(first, size + PAD)], [])
            there = [send_far(w0, 0)]
            sent = {s: partial(s, g_spans, BF16, [w0]) for s in far}
            got = {s: [chip_shift(part, s, f"grad{i}") for i, part in enumerate(sent[s])] for s in far}
            w_sib = core_swap(after(w, w0), "w_sib")
            (grad,) = partial(0, [(0, rows, 0)], F32, [sent[s][-1] for s in far])
            pieces = local_pieces(w_sib) + pieces_of(0, there[0], [grad])
            keys, back, *parts = project(pieces, own, cot, None, False, [grad], w_spans[1:])
            there += [send_far(part, 1 + i) for i, part in enumerate(parts)]
            state, order, ups, near = None, keys, [], []
            for i in range(len(g_spans)):
                *state, up, order = adam(i, state, [order])
                ups.append(up)
                near.append(rep_shift(order, distance, f"near{i}"))
            if heavy:
                updated = average(rows, g_spans[:1], ups[:1], near[:1], None, [order])
            else:
                updated = average(rows, g_spans, ups, near, None, [order])
            pieces = pieces_of(1, there[1], [updated]) + pieces_of(2, there[2], [updated])
            keys, back = project(pieces[:3], own, cot, (keys, back), False, [updated])
            keys, back = project(pieces[3:], own, cot, (keys, back), True, [])
            if heavy:
                updated = average(rows, g_spans[1:], ups[1:], near[1:], updated, [keys])
        else:
            g_spans = spans_of(rows, (13, 3))
            w_spans = [span[:2] for span in spans_of(rows, (1, 1))]
            sib, cot_sib, w_sib = core_swap(own, "hidden"), core_swap(cot, "cot"), core_swap(w, "w_sib")
            parts = cast_rows(w, w_spans, [])
            there = [send_far(part, i) for i, part in enumerate(parts)]
            sent = {s: partial(s, g_spans, BF16, [parts[0]]) for s in far}
            got = {s: [chip_shift(part, s, f"grad{i}") for i, part in enumerate(sent[s])] for s in far}
            keys, back = project(local_pieces(w_sib), own, cot, None, False, [sent[s][-1] for s in far])
            (grad,) = partial(0, [(0, rows, 0)], F32, [keys])
            pieces = [piece for i in range(len(there)) for piece in pieces_of(i, there[i], [grad])]
            keys, back = project(pieces, own, cot, (keys, back), True, [grad])
            state = adam(0, None, [keys])
            state = adam(1, state, [])
            updated = state[2]
        return keys, back, updated, state[0], state[1]

    return branch


def per_device(hidden, key_grad, weight, moment1, moment2, step):
    replicas = lax.axis_size("rep")
    distances = [2**level % replicas for level in range(LEVELS)]
    kinds = sorted(set(distances))
    level = lax.rem(step, LEVELS)
    pick = jnp.int32(0)
    for i, d in enumerate(distances):
        pick = jnp.where(level == i, kinds.index(d), pick)
    return lax.switch(
        pick, [make_branch(d) for d in kinds], hidden, key_grad, weight, moment1, moment2, step
    )


def solution(mesh):
    spec = P("rep", "fsdp", None)
    return jax.shard_map(
        per_device,
        mesh=mesh,
        in_specs=(spec,) * 5 + (P(),),
        out_specs=(spec,) * 5,
        check_vma=False,
    )
```

```python
import math

import jax
import jax.numpy as jnp
from jax import lax
from jax.experimental import pallas as pl
from jax.experimental.pallas import tpu as pltpu
from jax.sharding import PartitionSpec as P

LEVELS = 6
CORES = 2
PAD = 16
STRIP = 128
F32 = jnp.float32
BF16 = jnp.bfloat16
ANY = pl.BlockSpec(memory_space=pl.ANY)
HBM = pl.BlockSpec(memory_space=pltpu.HBM)
SMEM = pl.BlockSpec(memory_space=pltpu.SMEM)
VMEM = pl.BlockSpec(memory_space=pltpu.VMEM)
PARAMS = pltpu.CompilerParams(vmem_limit_bytes=16 * 2**20)
OVER_ROWS = (((0,), (0,)), ((), ()))
OVER_COLUMNS = (((1,), (1,)), ((), ()))


def call(kernel, name, **kwargs):
    with jax.named_scope("at_" + name):
        return pl.pallas_call(kernel, name=name, compiler_params=PARAMS, **kwargs)


def like(shape, dtype):
    return jax.ShapeDtypeStruct(shape, dtype)


def core_swap(value, name):
    n = lax.axis_size("fsdp")
    with jax.named_scope("at_" + name):
        return lax.ppermute(value, "fsdp", [(i, i ^ 1) for i in range(n)])


def chip_shift(value, distance, name):
    n = lax.axis_size("fsdp")
    with jax.named_scope("at_" + name):
        return lax.ppermute(value, "fsdp", [(i, (i + CORES * distance) % n) for i in range(n)])


def rep_shift(value, distance, name):
    n = lax.axis_size("rep")
    with jax.named_scope("at_" + name):
        return lax.ppermute(value, "rep", [((i - distance) % n, i) for i in range(n)])


def after(value, *done):
    return lax.optimization_barrier((value, *done))[0]


def shard_at(chip_step, other_core):
    n = lax.axis_size("fsdp")
    me = lax.axis_index("fsdp")
    core = lax.rem(me, CORES)
    if other_core:
        core = 1 - core
    return lax.rem(lax.div(me, CORES) + n // CORES - chip_step, n // CORES) * CORES + core


def spans_of(rows, shares, pads=None):
    unit = rows // sum(shares)
    pads = pads or (0,) * len(shares)
    return [(sum(shares[:i]) * unit, share * unit, pads[i]) for i, share in enumerate(shares)]


def strips_of(size):
    return [(at, min(STRIP, size - at)) for at in range(0, size, STRIP)]


def cast_rows(weight, spans, deps):
    kv = weight.shape[1]
    low, high = spans[0][0], sum(spans[-1])

    def kernel(src, *refs):
        buf, sem = refs[-2:]
        load = pltpu.make_async_copy(src.at[pl.ds(low, high - low), :], buf, sem)
        load.start()
        load.wait()
        for (first, size), out in zip(spans, refs[len(deps) :]):
            out[...] = buf[first - low : first - low + size, :].astype(BF16)

    return call(
        kernel,
        "cast",
        in_specs=[ANY] * (1 + len(deps)),
        out_specs=[VMEM] * len(spans),
        out_shape=[like((size, kv), BF16) for _, size in spans],
        scratch_shapes=[pltpu.VMEM((high - low, kv), F32), pltpu.SemaphoreType.DMA],
    )(weight, *deps)


def partial_grad(own, sib, cot, cot_sib, chip_step, spans, dtype, deps):
    kv = cot.shape[1]
    tokens = own.shape[0]
    rows = own.shape[1] // lax.axis_size("fsdp")

    def kernel(*refs):
        mine, theirs, cot_ref, cot_sib_ref = refs[:4]
        total = lax.dot_general(mine[...], cot_ref[...], OVER_ROWS, preferred_element_type=F32)
        total += lax.dot_general(theirs[...], cot_sib_ref[...], OVER_ROWS, preferred_element_type=F32)
        for (first, size, pad), out in zip(spans, refs[4 + len(deps) :]):
            out[:size, :] = total[first : first + size, :].astype(dtype)
            if pad:
                out[size:, :] = jnp.zeros((pad, kv), dtype)

    columns = pl.BlockSpec((tokens, rows), lambda g: (0, shard_at(chip_step, False)))
    whole = pl.BlockSpec((tokens, kv), lambda g: (0, 0))
    return call(
        kernel,
        "partial",
        grid=(1,),
        in_specs=[columns, columns, whole, whole] + [ANY] * len(deps),
        out_specs=[pl.BlockSpec((size + pad, kv), lambda g: (0, 0)) for _, size, pad in spans],
        out_shape=[like((size + pad, kv), dtype) for _, size, pad in spans],
    )(own, sib, cot, cot_sib, *deps)


def own_grad(own, sib, cot, cot_sib, held, step, deps):
    kv = cot.shape[1]
    tokens = own.shape[0]
    rows = own.shape[1] // lax.axis_size("fsdp")
    count = len(held)

    def kernel(*refs):
        step_ref, mine, theirs, cot_ref, cot_sib_ref = refs[:5]
        sources = refs[5 : 5 + count]
        out, scales, *places = refs[5 + count + len(deps) : -1]
        copies = [
            pltpu.make_async_copy(source, place, refs[-1].at[i])
            for i, (source, place) in enumerate(zip(sources, places))
        ]
        for copy in copies:
            copy.start()
        total = lax.dot_general(mine[...], cot_ref[...], OVER_ROWS, preferred_element_type=F32)
        total += lax.dot_general(theirs[...], cot_sib_ref[...], OVER_ROWS, preferred_element_type=F32)
        out[...] = total
        time = jnp.full((8, kv), (step_ref[0] + 1).astype(F32))
        for i, decay in enumerate((0.9, 0.95)):
            scales[8 * i : 8 * (i + 1), :] = 1.0 / (1.0 - jnp.exp(time * math.log(decay)))
        for copy in copies:
            copy.wait()

    columns = pl.BlockSpec((tokens, rows), lambda g: (0, shard_at(0, False)))
    whole = pl.BlockSpec((tokens, kv), lambda g: (0, 0))
    return call(
        kernel,
        "own_grad",
        grid=(1,),
        in_specs=[SMEM, columns, columns, whole, whole] + [ANY] * (count + len(deps)),
        out_specs=[VMEM] * (2 + count),
        out_shape=[pltpu.VMEM((rows, kv), F32), pltpu.VMEM((16, kv), F32)]
        + [pltpu.VMEM(array.shape, array.dtype) for array in held],
        scratch_shapes=[pltpu.SemaphoreType.DMA((count,))],
    )(step.reshape(1), own, sib, cot, cot_sib, *held, *deps)


def adam_rows(span, grad, got, weight, moments, scales, so_far, send, deps):
    first, size, pad = span
    rows, kv = weight.shape
    count = len(got)
    kept = 2 if send else 3
    strips = strips_of(size)

    def kernel(*refs):
        scales_ref, grad_ref = refs[:2]
        got_refs = refs[2 : 2 + count]
        w_ref, m_ref, v_ref = refs[2 + count : 5 + count]
        at = 5 + count + (kept if so_far else 0) + len(deps)
        places = refs[at : at + kept]
        at += kept
        if send:
            up_out, short_out = refs[at : at + 2]
            at += 2
        bufs, sems = refs[at : at + kept], refs[at + kept]
        copies = []
        scale1, scale2 = scales_ref[:1, :], scales_ref[8:9, :]
        for i, (strip, high) in enumerate(strips):
            here = slice(strip, strip + high)
            there = slice(first + strip, first + strip + high)
            g = grad_ref[there, :]
            for ref in got_refs:
                g += ref[here, :].astype(F32)
            w = w_ref[there, :]
            m = 0.9 * m_ref[there, :].astype(F32) + 0.1 * g
            v = 0.95 * v_ref[there, :].astype(F32) + 0.05 * g * g
            up = w - 0.003 * ((m * scale1) / (jnp.sqrt(v * scale2) + 1e-8) + 0.1 * w)
            bufs[0][here, :] = m.astype(BF16)
            bufs[1][here, :] = v.astype(BF16)
            if send:
                up_out[here, :] = up
                short_out[here, :] = up.astype(BF16)
            else:
                bufs[2][here, :] = up
            for j in range(kept):
                copies.append(
                    pltpu.make_async_copy(
                        bufs[j].at[pl.ds(strip, high), :],
                        places[j].at[0, pl.ds(first + strip, high), :],
                        sems.at[j, i],
                    )
                )
                copies[-1].start()
        if send and pad:
            short_out[size:, :] = jnp.zeros((pad, kv), BF16)
        for copy in copies:
            copy.wait()

    kinds = [BF16, BF16] + ([] if send else [F32])
    return call(
        kernel,
        "adam",
        in_specs=[VMEM] * (5 + count) + [HBM] * (kept if so_far else 0) + [ANY] * len(deps),
        out_specs=[HBM] * kept + ([VMEM, VMEM] if send else []),
        out_shape=[pltpu.HBM((1, rows, kv), kind) for kind in kinds]
        + ([like((size, kv), F32), like((size + pad, kv), BF16)] if send else []),
        scratch_shapes=[pltpu.VMEM((size, kv), kind) for kind in kinds]
        + [pltpu.SemaphoreType.DMA((kept, len(strips)))],
        input_output_aliases={5 + count + i: i for i in range(kept)} if so_far else {},
    )(scales, grad, *got, weight, *moments, *(so_far or ()), *deps)


def project(pieces, own, cot, so_far, last, deps, emit=()):
    tokens, width = own.shape
    kv = cot.shape[1]
    shard = width // lax.axis_size("fsdp")
    count = len(pieces)
    sizes = [piece[1] for piece in pieces]

    def kernel(*refs):
        weights, (cot_ref, own_ref) = refs[:count], refs[count : count + 2]
        at = count + 2
        if so_far:
            keys_ref = refs[at]
            at += 2
        at += len(deps)
        keys_out, back_out = refs[at : at + 2]
        spans_out = refs[at + 2 : at + 2 + len(emit)]
        at += 2 + len(emit)
        outs, shorts = refs[at : at + count], refs[at + count : at + count + len(emit)]
        keys_buf, sems = refs[-2:]
        stores = []
        for i, ((first, size), out) in enumerate(zip(emit, spans_out)):
            shorts[i][...] = weights[0][first : first + size, :].astype(BF16)
            stores.append(pltpu.make_async_copy(shorts[i], out, sems.at[count + 1 + i]))
            stores[-1].start()
        total = keys_ref[...] if so_far else None
        for j, (_, _, steps, other, first) in enumerate(pieces):
            place = pl.ds(pl.multiple_of(shard_at(steps, other) * shard + first, 128), sizes[j])
            rows = weights[j][: sizes[j], :].astype(BF16)
            outs[j][...] = lax.dot_general(
                cot_ref[...], rows, OVER_COLUMNS, preferred_element_type=F32
            ).astype(BF16)
            stores.append(pltpu.make_async_copy(outs[j], back_out.at[0, :, place], sems.at[j]))
            stores[-1].start()
            term = jnp.dot(own_ref[:, place], rows, preferred_element_type=F32)
            total = term if total is None else total + term
        if last:
            keys_buf[...] = total.astype(BF16)
            stores.append(pltpu.make_async_copy(keys_buf, keys_out.at[0], sems.at[count]))
            stores[-1].start()
        else:
            keys_out[...] = total
        for store in stores:
            store.wait()

    return call(
        kernel,
        "project",
        in_specs=[VMEM] * (count + 2) + ([VMEM, HBM] if so_far else []) + [ANY] * len(deps),
        out_specs=[HBM if last else VMEM, HBM] + [HBM] * len(emit),
        out_shape=[
            pltpu.HBM((1, tokens, kv), BF16) if last else like((tokens, kv), F32),
            pltpu.HBM((1, tokens, width), BF16),
        ]
        + [pltpu.HBM((size, kv), BF16) for _, size in emit],
        scratch_shapes=[pltpu.VMEM((tokens, size), BF16) for size in sizes]
        + [pltpu.VMEM((size, kv), BF16) for _, size in emit]
        + [pltpu.VMEM((tokens, kv), BF16), pltpu.SemaphoreType.DMA((count + 1 + len(emit),))],
        input_output_aliases={count + 3: 1} if so_far else {},
    )(*[piece[0] for piece in pieces], cot, own, *(so_far or ()), *deps)


def average(rows, spans, updated, neighbours, so_far, deps):
    kv = updated[0].shape[1]
    count = len(spans)
    strips = [(j, first, *strip) for j, (first, size, _) in enumerate(spans) for strip in strips_of(size)]

    def kernel(*refs):
        out, buf, sems = refs[-3:]
        copies = []
        for i, (j, first, strip, high) in enumerate(strips):
            here = slice(strip, strip + high)
            at = pl.ds(first - spans[0][0] + strip, high)
            buf[at, :] = 0.5 * (refs[j][here, :] + refs[count + j][here, :].astype(F32))
            copies.append(
                pltpu.make_async_copy(buf.at[at, :], out.at[0, pl.ds(first + strip, high), :], sems.at[i])
            )
            copies[-1].start()
        for copy in copies:
            copy.wait()

    before = [] if so_far is None else [so_far]
    return call(
        kernel,
        "average",
        in_specs=[VMEM] * (2 * count) + [HBM] * len(before) + [ANY] * len(deps),
        out_specs=HBM,
        out_shape=pltpu.HBM((1, rows, kv), F32),
        scratch_shapes=[
            pltpu.VMEM((sum(size for _, size, _ in spans), kv), F32),
            pltpu.SemaphoreType.DMA((len(strips),)),
        ],
        input_output_aliases={2 * count: 0} if before else {},
    )(*updated, *neighbours, *before, *deps)


def make_branch(distance):
    def branch(hidden, key_grad, weight, moment1, moment2, step):
        chips = lax.axis_size("fsdp") // CORES
        own, cot, w = hidden[0], key_grad[0], weight[0]
        state_in = (w, moment1[0], moment2[0])
        rows = w.shape[0]
        far = range(1, chips)

        def local_pieces(w_sib):
            return [(held[0], rows, 0, False, 0), (w_sib, rows, 0, True, 0)]

        def send_far(part, i):
            return [chip_shift(part, s, f"far{i}") for s in far]

        def pieces_of(i, arrays, order):
            first, size = w_spans[i]
            return [(v, size, s, False, first) for v, s in zip(arrays, far)] + [
                (core_swap(after(v, *order), f"swap{i}"), size, s, True, first) for v, s in zip(arrays, far)
            ]

        def adam(i, state, deps):
            return adam_rows(
                g_spans[i], grad, [got[s][i] for s in far], held[0], held[1:], scales, state, bool(distance), deps
            )

        def partial(s, spans, dtype, deps):
            return partial_grad(own, sib, cot, cot_sib, -s % chips, spans, dtype, deps)

        if 2 * distance >= lax.axis_size("rep"):
            g_spans = spans_of(rows, (25, 39))
            w_spans = [span[:2] for span in spans_of(rows, (1, 1))]
            sib, cot_sib = core_swap(own, "hidden"), core_swap(cot, "cot")
            sent = {s: partial(s, g_spans, BF16, []) for s in far}
            got = {s: [chip_shift(part, s, f"grad{i}") for i, part in enumerate(sent[s])] for s in far}
            w_sib = core_swap(after(w, *[sent[s][-1] for s in far]), "w_sib")
            grad, scales, *held = own_grad(own, sib, cot, cot_sib, state_in, step, [sent[s][-1] for s in far])
            keys, back, *parts = project(local_pieces(w_sib), own, cot, None, False, [grad], w_spans)
            there = [send_far(part, i) for i, part in enumerate(parts)]
            ups, shorts = [], []
            *state, up, short = adam(0, None, [keys])
            ups.append(up)
            near = [rep_shift(short, distance, "near0")]
            *state, up, short = adam(1, state, [short])
            ups.append(up)
            near.append(rep_shift(short, distance, "near1"))
            updated = average(rows, g_spans[:1], ups[:1], near[:1], None, [short])
            pieces = [piece for i in range(len(there)) for piece in pieces_of(i, there[i], [updated])]
            keys, back = project(pieces, own, cot, (keys, back), True, [updated])
            updated = average(rows, g_spans[1:], ups[1:], near[1:], updated, [keys])
        elif distance:
            g_spans = spans_of(rows, (25, 20, 19))
            w_spans = [span[:2] for span in spans_of(rows, (2, 3, 3))]
            sent_spans = [(w_spans[i][0], w_spans[i][1] + pad) for i, pad in enumerate((PAD, PAD, 0))]
            sib, cot_sib = core_swap(own, "hidden"), core_swap(cot, "cot")
            (w0,) = cast_rows(w, sent_spans[:1], [])
            there = [send_far(w0, 0)]
            sent = {s: partial(s, g_spans, BF16, [w0]) for s in far}
            got = {s: [chip_shift(part, s, f"grad{i}") for i, part in enumerate(sent[s])] for s in far}
            w_sib = core_swap(after(w, w0), "w_sib")
            grad, scales, *held = own_grad(own, sib, cot, cot_sib, state_in, step, [sent[s][-1] for s in far])
            pieces = local_pieces(w_sib) + pieces_of(0, there[0], [grad])
            keys, back, *parts = project(pieces, own, cot, None, False, [grad], sent_spans[1:])
            there += [send_far(part, 1 + i) for i, part in enumerate(parts)]
            state, order, ups, near = None, keys, [], []
            for i in range(len(g_spans)):
                *state, up, order = adam(i, state, [order])
                ups.append(up)
                near.append(rep_shift(order, distance, f"near{i}"))
            updated = average(rows, g_spans, ups, near, None, [order])
            pieces = pieces_of(1, there[1], [order]) + pieces_of(2, there[2], [updated])
            last = len(far)
            keys, back = project(pieces[:-last], own, cot, (keys, back), False, [updated])
            keys, back = project(pieces[-last:], own, cot, (keys, back), True, [])
        else:
            g_spans = spans_of(rows, (13, 3))
            w_spans = [span[:2] for span in spans_of(rows, (1, 1))]
            sib, cot_sib, w_sib = core_swap(own, "hidden"), core_swap(cot, "cot"), core_swap(w, "w_sib")
            parts = cast_rows(w, w_spans, [])
            there = [send_far(part, i) for i, part in enumerate(parts)]
            sent = {s: partial(s, g_spans, BF16, [parts[0]]) for s in far}
            got = {s: [chip_shift(part, s, f"grad{i}") for i, part in enumerate(sent[s])] for s in far}
            grad, scales, *held = own_grad(own, sib, cot, cot_sib, state_in, step, [sent[s][-1] for s in far])
            keys, back = project(local_pieces(w_sib), own, cot, None, False, [grad])
            pieces = [piece for i in range(len(there)) for piece in pieces_of(i, there[i], [keys])]
            keys, back = project(pieces, own, cot, (keys, back), True, [keys])
            state = adam(0, None, [keys])
            state = adam(1, state, [])
            updated = state[2]
        return keys, back, updated, state[0], state[1]

    return branch


def per_device(hidden, key_grad, weight, moment1, moment2, step):
    replicas = lax.axis_size("rep")
    distances = [2**level % replicas for level in range(LEVELS)]
    kinds = sorted(set(distances))
    level = lax.rem(step, LEVELS)
    pick = jnp.int32(0)
    for i, d in enumerate(distances):
        pick = jnp.where(level == i, kinds.index(d), pick)
    return lax.switch(
        pick, [make_branch(d) for d in kinds], hidden, key_grad, weight, moment1, moment2, step
    )


def solution(mesh):
    spec = P("rep", "fsdp", None)
    return jax.shard_map(
        per_device,
        mesh=mesh,
        in_specs=(spec,) * 5 + (P(),),
        out_specs=(spec,) * 5,
        check_vma=False,
    )
```

```python
import math

import jax
import jax.numpy as jnp
from jax import lax
from jax.experimental import pallas as pl
from jax.experimental.pallas import tpu as pltpu
from jax.sharding import PartitionSpec as P

LEVELS = 6
CORES = 2
PAD = 16
STRIP = 128
F32 = jnp.float32
BF16 = jnp.bfloat16
ANY = pl.BlockSpec(memory_space=pl.ANY)
HBM = pl.BlockSpec(memory_space=pltpu.HBM)
SMEM = pl.BlockSpec(memory_space=pltpu.SMEM)
VMEM = pl.BlockSpec(memory_space=pltpu.VMEM)
PARAMS = pltpu.CompilerParams(vmem_limit_bytes=16 * 2**20)
OVER_ROWS = (((0,), (0,)), ((), ()))
OVER_COLUMNS = (((1,), (1,)), ((), ()))


def call(kernel, name, **kwargs):
    with jax.named_scope("at_" + name):
        return pl.pallas_call(kernel, name=name, compiler_params=PARAMS, **kwargs)


def like(shape, dtype):
    return jax.ShapeDtypeStruct(shape, dtype)


def core_swap(value, name):
    n = lax.axis_size("fsdp")
    with jax.named_scope("at_" + name):
        return lax.ppermute(value, "fsdp", [(i, i ^ 1) for i in range(n)])


def chip_shift(value, distance, name):
    n = lax.axis_size("fsdp")
    with jax.named_scope("at_" + name):
        return lax.ppermute(value, "fsdp", [(i, (i + CORES * distance) % n) for i in range(n)])


def rep_shift(value, distance, name):
    n = lax.axis_size("rep")
    with jax.named_scope("at_" + name):
        return lax.ppermute(value, "rep", [((i - distance) % n, i) for i in range(n)])


def after(value, *done):
    return lax.optimization_barrier((value, *done))[0]


def shard_at(chip_step, other_core):
    n = lax.axis_size("fsdp")
    me = lax.axis_index("fsdp")
    core = lax.rem(me, CORES)
    if other_core:
        core = 1 - core
    return lax.rem(lax.div(me, CORES) + n // CORES - chip_step, n // CORES) * CORES + core


def spans_of(rows, shares, pads=None):
    unit = rows // sum(shares)
    pads = pads or (0,) * len(shares)
    return [(sum(shares[:i]) * unit, share * unit, pads[i]) for i, share in enumerate(shares)]


def strips_of(size):
    return [(at, min(STRIP, size - at)) for at in range(0, size, STRIP)]


def cast_rows(weight, spans, deps):
    kv = weight.shape[1]
    low, high = spans[0][0], sum(spans[-1])

    def kernel(src, *refs):
        buf, sem = refs[-2:]
        load = pltpu.make_async_copy(src.at[pl.ds(low, high - low), :], buf, sem)
        load.start()
        load.wait()
        for (first, size), out in zip(spans, refs[len(deps) :]):
            out[...] = buf[first - low : first - low + size, :].astype(BF16)

    return call(
        kernel,
        "cast",
        in_specs=[ANY] * (1 + len(deps)),
        out_specs=[VMEM] * len(spans),
        out_shape=[like((size, kv), BF16) for _, size in spans],
        scratch_shapes=[pltpu.VMEM((high - low, kv), F32), pltpu.SemaphoreType.DMA],
    )(weight, *deps)


def partial_grad(own, sib, cot, cot_sib, chip_step, spans, dtype, deps):
    kv = cot.shape[1]
    tokens = own.shape[0]
    rows = own.shape[1] // lax.axis_size("fsdp")

    def kernel(*refs):
        mine, theirs, cot_ref, cot_sib_ref = refs[:4]
        total = lax.dot_general(mine[...], cot_ref[...], OVER_ROWS, preferred_element_type=F32)
        total += lax.dot_general(theirs[...], cot_sib_ref[...], OVER_ROWS, preferred_element_type=F32)
        for (first, size, pad), out in zip(spans, refs[4 + len(deps) :]):
            out[:size, :] = total[first : first + size, :].astype(dtype)
            if pad:
                out[size:, :] = jnp.zeros((pad, kv), dtype)

    columns = pl.BlockSpec((tokens, rows), lambda g: (0, shard_at(chip_step, False)))
    whole = pl.BlockSpec((tokens, kv), lambda g: (0, 0))
    return call(
        kernel,
        "partial",
        grid=(1,),
        in_specs=[columns, columns, whole, whole] + [ANY] * len(deps),
        out_specs=[pl.BlockSpec((size + pad, kv), lambda g: (0, 0)) for _, size, pad in spans],
        out_shape=[like((size + pad, kv), dtype) for _, size, pad in spans],
    )(own, sib, cot, cot_sib, *deps)


def own_grad(own, sib, cot, cot_sib, held, step, deps):
    kv = cot.shape[1]
    tokens = own.shape[0]
    rows = own.shape[1] // lax.axis_size("fsdp")
    count = len(held)

    def kernel(*refs):
        step_ref, mine, theirs, cot_ref, cot_sib_ref = refs[:5]
        sources = refs[5 : 5 + count]
        out, scales, *places = refs[5 + count + len(deps) : -1]
        copies = [
            pltpu.make_async_copy(source, place, refs[-1].at[i])
            for i, (source, place) in enumerate(zip(sources, places))
        ]
        for copy in copies:
            copy.start()
        total = lax.dot_general(mine[...], cot_ref[...], OVER_ROWS, preferred_element_type=F32)
        total += lax.dot_general(theirs[...], cot_sib_ref[...], OVER_ROWS, preferred_element_type=F32)
        out[...] = total
        time = jnp.full((8, kv), (step_ref[0] + 1).astype(F32))
        for i, decay in enumerate((0.9, 0.95)):
            scales[8 * i : 8 * (i + 1), :] = 1.0 / (1.0 - jnp.exp(time * math.log(decay)))
        for copy in copies:
            copy.wait()

    columns = pl.BlockSpec((tokens, rows), lambda g: (0, shard_at(0, False)))
    whole = pl.BlockSpec((tokens, kv), lambda g: (0, 0))
    return call(
        kernel,
        "own_grad",
        grid=(1,),
        in_specs=[SMEM, columns, columns, whole, whole] + [ANY] * (count + len(deps)),
        out_specs=[VMEM] * (2 + count),
        out_shape=[pltpu.VMEM((rows, kv), F32), pltpu.VMEM((16, kv), F32)]
        + [pltpu.VMEM(array.shape, array.dtype) for array in held],
        scratch_shapes=[pltpu.SemaphoreType.DMA((count,))],
    )(step.reshape(1), own, sib, cot, cot_sib, *held, *deps)


def adam_rows(span, grad, got, weight, moments, scales, so_far, send, deps):
    first, size, pad = span
    rows, kv = weight.shape
    count = len(got)
    kept = 2 if send else 3
    strips = strips_of(size)

    def kernel(*refs):
        scales_ref, grad_ref = refs[:2]
        got_refs = refs[2 : 2 + count]
        w_ref, m_ref, v_ref = refs[2 + count : 5 + count]
        at = 5 + count + (kept if so_far else 0) + len(deps)
        places = refs[at : at + kept]
        at += kept
        if send:
            up_out, short_out = refs[at : at + 2]
            at += 2
        bufs, sems = refs[at : at + kept], refs[at + kept]
        copies = []
        scale1, scale2 = scales_ref[:1, :], scales_ref[8:9, :]
        for i, (strip, high) in enumerate(strips):
            here = slice(strip, strip + high)
            there = slice(first + strip, first + strip + high)
            g = grad_ref[there, :]
            for ref in got_refs:
                g += ref[here, :].astype(F32)
            w = w_ref[there, :]
            m = 0.9 * m_ref[there, :].astype(F32) + 0.1 * g
            v = 0.95 * v_ref[there, :].astype(F32) + 0.05 * g * g
            up = w - 0.003 * ((m * scale1) / (jnp.sqrt(v * scale2) + 1e-8) + 0.1 * w)
            bufs[0][here, :] = m.astype(BF16)
            bufs[1][here, :] = v.astype(BF16)
            if send:
                up_out[here, :] = up
                short_out[here, :] = up.astype(BF16)
            else:
                bufs[2][here, :] = up
            for j in range(kept):
                copies.append(
                    pltpu.make_async_copy(
                        bufs[j].at[pl.ds(strip, high), :],
                        places[j].at[0, pl.ds(first + strip, high), :],
                        sems.at[j, i],
                    )
                )
                copies[-1].start()
        if send and pad:
            short_out[size:, :] = jnp.zeros((pad, kv), BF16)
        for copy in copies:
            copy.wait()

    kinds = [BF16, BF16] + ([] if send else [F32])
    return call(
        kernel,
        "adam",
        in_specs=[VMEM] * (5 + count) + [HBM] * (kept if so_far else 0) + [ANY] * len(deps),
        out_specs=[HBM] * kept + ([VMEM, VMEM] if send else []),
        out_shape=[pltpu.HBM((1, rows, kv), kind) for kind in kinds]
        + ([like((size, kv), F32), like((size + pad, kv), BF16)] if send else []),
        scratch_shapes=[pltpu.VMEM((size, kv), kind) for kind in kinds]
        + [pltpu.SemaphoreType.DMA((kept, len(strips)))],
        input_output_aliases={5 + count + i: i for i in range(kept)} if so_far else {},
    )(scales, grad, *got, weight, *moments, *(so_far or ()), *deps)


def project(pieces, own, cot, so_far, last, deps, emit=()):
    tokens, width = own.shape
    kv = cot.shape[1]
    shard = width // lax.axis_size("fsdp")
    count = len(pieces)
    sizes = [piece[1] for piece in pieces]

    def kernel(*refs):
        weights, (cot_ref, own_ref) = refs[:count], refs[count : count + 2]
        at = count + 2
        if so_far:
            keys_ref = refs[at]
            at += 2
        at += len(deps)
        keys_out, back_out = refs[at : at + 2]
        spans_out = refs[at + 2 : at + 2 + len(emit)]
        at += 2 + len(emit)
        outs, shorts = refs[at : at + count], refs[at + count : at + count + len(emit)]
        keys_buf, sems = refs[-2:]
        stores = []
        for i, ((first, size), out) in enumerate(zip(emit, spans_out)):
            shorts[i][...] = weights[0][first : first + size, :].astype(BF16)
            stores.append(pltpu.make_async_copy(shorts[i], out, sems.at[count + 1 + i]))
            stores[-1].start()
        total = keys_ref[...] if so_far else None
        for j, (_, _, steps, other, first) in enumerate(pieces):
            place = pl.ds(pl.multiple_of(shard_at(steps, other) * shard + first, 128), sizes[j])
            rows = weights[j][: sizes[j], :].astype(BF16)
            outs[j][...] = lax.dot_general(
                cot_ref[...], rows, OVER_COLUMNS, preferred_element_type=F32
            ).astype(BF16)
            stores.append(pltpu.make_async_copy(outs[j], back_out.at[0, :, place], sems.at[j]))
            stores[-1].start()
            term = jnp.dot(own_ref[:, place], rows, preferred_element_type=F32)
            total = term if total is None else total + term
        if last:
            keys_buf[...] = total.astype(BF16)
            stores.append(pltpu.make_async_copy(keys_buf, keys_out.at[0], sems.at[count]))
            stores[-1].start()
        else:
            keys_out[...] = total
        for store in stores:
            store.wait()

    return call(
        kernel,
        "project",
        in_specs=[VMEM] * (count + 2) + ([VMEM, HBM] if so_far else []) + [ANY] * len(deps),
        out_specs=[HBM if last else VMEM, HBM] + [HBM] * len(emit),
        out_shape=[
            pltpu.HBM((1, tokens, kv), BF16) if last else like((tokens, kv), F32),
            pltpu.HBM((1, tokens, width), BF16),
        ]
        + [pltpu.HBM((size, kv), BF16) for _, size in emit],
        scratch_shapes=[pltpu.VMEM((tokens, size), BF16) for size in sizes]
        + [pltpu.VMEM((size, kv), BF16) for _, size in emit]
        + [pltpu.VMEM((tokens, kv), BF16), pltpu.SemaphoreType.DMA((count + 1 + len(emit),))],
        input_output_aliases={count + 3: 1} if so_far else {},
    )(*[piece[0] for piece in pieces], cot, own, *(so_far or ()), *deps)


def average(rows, spans, updated, neighbours, so_far, deps):
    kv = updated[0].shape[1]
    count = len(spans)
    strips = [(j, first, *strip) for j, (first, size, _) in enumerate(spans) for strip in strips_of(size)]

    def kernel(*refs):
        out, buf, sems = refs[-3:]
        copies = []
        for i, (j, first, strip, high) in enumerate(strips):
            here = slice(strip, strip + high)
            at = pl.ds(first - spans[0][0] + strip, high)
            buf[at, :] = 0.5 * (refs[j][here, :] + refs[count + j][here, :].astype(F32))
            copies.append(
                pltpu.make_async_copy(buf.at[at, :], out.at[0, pl.ds(first + strip, high), :], sems.at[i])
            )
            copies[-1].start()
        for copy in copies:
            copy.wait()

    before = [] if so_far is None else [so_far]
    return call(
        kernel,
        "average",
        in_specs=[VMEM] * (2 * count) + [HBM] * len(before) + [ANY] * len(deps),
        out_specs=HBM,
        out_shape=pltpu.HBM((1, rows, kv), F32),
        scratch_shapes=[
            pltpu.VMEM((sum(size for _, size, _ in spans), kv), F32),
            pltpu.SemaphoreType.DMA((len(strips),)),
        ],
        input_output_aliases={2 * count: 0} if before else {},
    )(*updated, *neighbours, *before, *deps)


def make_branch(distance):
    def branch(hidden, key_grad, weight, moment1, moment2, step):
        chips = lax.axis_size("fsdp") // CORES
        own, cot, w = hidden[0], key_grad[0], weight[0]
        state_in = (w, moment1[0], moment2[0])
        rows = w.shape[0]
        far = range(1, chips)

        def local_pieces(w_sib):
            return [(held[0], rows, 0, False, 0), (w_sib, rows, 0, True, 0)]

        def send_far(part, i):
            return [chip_shift(part, s, f"far{i}") for s in far]

        def pieces_of(i, arrays, order):
            first, size = w_spans[i]
            return [(v, size, s, False, first) for v, s in zip(arrays, far)] + [
                (core_swap(after(v, *order), f"swap{i}"), size, s, True, first) for v, s in zip(arrays, far)
            ]

        def adam(i, state, deps):
            return adam_rows(
                g_spans[i], grad, [got[s][i] for s in far], held[0], held[1:], scales, state, bool(distance), deps
            )

        def partial(s, spans, dtype, deps):
            return partial_grad(own, sib, cot, cot_sib, -s % chips, spans, dtype, deps)

        if 2 * distance >= lax.axis_size("rep"):
            g_spans = spans_of(rows, (20, 19, 25))
            w_spans = [span[:2] for span in spans_of(rows, (3, 3, 2))]
            sib, cot_sib = core_swap(own, "hidden"), core_swap(cot, "cot")
            sent = {s: partial(s, g_spans, BF16, []) for s in far}
            got = {s: [chip_shift(part, s, f"grad{i}") for i, part in enumerate(sent[s])] for s in far}
            w_sib = core_swap(after(w, *[sent[s][-1] for s in far]), "w_sib")
            grad, scales, *held = own_grad(own, sib, cot, cot_sib, state_in, step, [sent[s][-1] for s in far])
            keys, back, *parts = project(local_pieces(w_sib), own, cot, None, False, [grad], w_spans)
            there = [send_far(part, i) for i, part in enumerate(parts)]
            state, order, updated, ups, near = None, keys, None, [], []
            for i in range(len(g_spans)):
                if i > 1:
                    updated = order = average(rows, [g_spans[i - 2]], [ups[i - 2]], [near[i - 2]], updated, [order])
                *state, up, order = adam(i, state, [order])
                ups.append(up)
                near.append(rep_shift(order, distance, f"near{i}"))
            updated = average(rows, [g_spans[-2]], [ups[-2]], [near[-2]], updated, [order])
            pieces = [piece for i in range(len(there)) for piece in pieces_of(i, there[i], [updated])]
            keys, back = project(pieces, own, cot, (keys, back), True, [updated])
            updated = average(rows, [g_spans[-1]], [ups[-1]], [near[-1]], updated, [keys])
        elif distance:
            g_spans = spans_of(rows, (25, 20, 19))
            w_spans = [span[:2] for span in spans_of(rows, (2, 3, 3))]
            sent_spans = [(w_spans[i][0], w_spans[i][1] + pad) for i, pad in enumerate((PAD, PAD, 0))]
            sib, cot_sib = core_swap(own, "hidden"), core_swap(cot, "cot")
            (w0,) = cast_rows(w, sent_spans[:1], [])
            there = [send_far(w0, 0)]
            sent = {s: partial(s, g_spans, BF16, [w0]) for s in far}
            got = {s: [chip_shift(part, s, f"grad{i}") for i, part in enumerate(sent[s])] for s in far}
            w_sib = core_swap(after(w, w0), "w_sib")
            grad, scales, *held = own_grad(own, sib, cot, cot_sib, state_in, step, [sent[s][-1] for s in far])
            pieces = local_pieces(w_sib) + pieces_of(0, there[0], [grad])
            keys, back, *parts = project(pieces, own, cot, None, False, [grad], sent_spans[1:])
            there += [send_far(part, 1 + i) for i, part in enumerate(parts)]
            state, order, ups, near = None, keys, [], []
            for i in range(len(g_spans)):
                *state, up, order = adam(i, state, [order])
                ups.append(up)
                near.append(rep_shift(order, distance, f"near{i}"))
            updated = average(rows, g_spans, ups, near, None, [order])
            pieces = pieces_of(1, there[1], [order]) + pieces_of(2, there[2], [updated])
            last = len(far)
            keys, back = project(pieces[:-last], own, cot, (keys, back), False, [updated])
            keys, back = project(pieces[-last:], own, cot, (keys, back), True, [])
        else:
            g_spans = spans_of(rows, (13, 3))
            w_spans = [span[:2] for span in spans_of(rows, (1, 1))]
            sib, cot_sib, w_sib = core_swap(own, "hidden"), core_swap(cot, "cot"), core_swap(w, "w_sib")
            parts = cast_rows(w, w_spans, [])
            there = [send_far(part, i) for i, part in enumerate(parts)]
            sent = {s: partial(s, g_spans, BF16, [parts[0]]) for s in far}
            got = {s: [chip_shift(part, s, f"grad{i}") for i, part in enumerate(sent[s])] for s in far}
            grad, scales, *held = own_grad(own, sib, cot, cot_sib, state_in, step, [sent[s][-1] for s in far])
            keys, back = project(local_pieces(w_sib), own, cot, None, False, [grad])
            pieces = [piece for i in range(len(there)) for piece in pieces_of(i, there[i], [keys])]
            keys, back = project(pieces, own, cot, (keys, back), True, [keys])
            state = adam(0, None, [keys])
            state = adam(1, state, [])
            updated = state[2]
        return keys, back, updated, state[0], state[1]

    return branch


def per_device(hidden, key_grad, weight, moment1, moment2, step):
    replicas = lax.axis_size("rep")
    distances = [2**level % replicas for level in range(LEVELS)]
    kinds = sorted(set(distances))
    level = lax.rem(step, LEVELS)
    pick = jnp.int32(0)
    for i, d in enumerate(distances):
        pick = jnp.where(level == i, kinds.index(d), pick)
    return lax.switch(
        pick, [make_branch(d) for d in kinds], hidden, key_grad, weight, moment1, moment2, step
    )


def solution(mesh):
    spec = P("rep", "fsdp", None)
    return jax.shard_map(
        per_device,
        mesh=mesh,
        in_specs=(spec,) * 5 + (P(),),
        out_specs=(spec,) * 5,
        check_vma=False,
    )
```

```python
import math

import jax
import jax.numpy as jnp
from jax import lax
from jax.experimental import pallas as pl
from jax.experimental.pallas import tpu as pltpu
from jax.sharding import PartitionSpec as P

LEVELS = 6
CORES = 2
PAD = 16
STRIP = 128
F32 = jnp.float32
BF16 = jnp.bfloat16
ANY = pl.BlockSpec(memory_space=pl.ANY)
HBM = pl.BlockSpec(memory_space=pltpu.HBM)
SMEM = pl.BlockSpec(memory_space=pltpu.SMEM)
VMEM = pl.BlockSpec(memory_space=pltpu.VMEM)
PARAMS = pltpu.CompilerParams(vmem_limit_bytes=16 * 2**20)
OVER_ROWS = (((0,), (0,)), ((), ()))
OVER_COLUMNS = (((1,), (1,)), ((), ()))


def call(kernel, name, **kwargs):
    with jax.named_scope(name):
        return pl.pallas_call(kernel, name=name, compiler_params=PARAMS, **kwargs)


def like(shape, dtype):
    return jax.ShapeDtypeStruct(shape, dtype)


def core_swap(value, name):
    n = lax.axis_size("fsdp")
    with jax.named_scope(name):
        return lax.ppermute(value, "fsdp", [(i, i ^ 1) for i in range(n)])


def chip_shift(value, distance, name):
    n = lax.axis_size("fsdp")
    with jax.named_scope(name):
        return lax.ppermute(value, "fsdp", [(i, (i + CORES * distance) % n) for i in range(n)])


def rep_shift(value, distance, name):
    n = lax.axis_size("rep")
    with jax.named_scope(name):
        return lax.ppermute(value, "rep", [((i - distance) % n, i) for i in range(n)])


def after(value, *done):
    return lax.optimization_barrier((value, *done))[0]


def shard_at(chip_step, other_core):
    n = lax.axis_size("fsdp")
    me = lax.axis_index("fsdp")
    core = lax.rem(me, CORES)
    if other_core:
        core = 1 - core
    return lax.rem(lax.div(me, CORES) + n // CORES - chip_step, n // CORES) * CORES + core


def spans_of(rows, shares, pads=None):
    unit = rows // sum(shares)
    pads = pads or (0,) * len(shares)
    return [(sum(shares[:i]) * unit, share * unit, pads[i]) for i, share in enumerate(shares)]


def strips_of(size):
    return [(at, min(STRIP, size - at)) for at in range(0, size, STRIP)]


def cast_rows(weight, spans, deps):
    kv = weight.shape[1]
    low, high = spans[0][0], sum(spans[-1])

    cuts = [(first + at, high) for first, size in spans for at, high in strips_of(size)]

    def kernel(src, *refs):
        buf, sems = refs[-2:]
        loads = [
            pltpu.make_async_copy(
                src.at[pl.ds(at, high), :], buf.at[pl.ds(at - low, high), :], sems.at[i]
            )
            for i, (at, high) in enumerate(cuts)
        ]
        for load in loads:
            load.start()
        loads = iter(loads)
        for (first, size), out in zip(spans, refs[len(deps) :]):
            for at, high in strips_of(size):
                next(loads).wait()
                here = first - low + at
                out[at : at + high, :] = buf[here : here + high, :].astype(BF16)

    return call(
        kernel,
        "cast",
        in_specs=[ANY] * (1 + len(deps)),
        out_specs=[VMEM] * len(spans),
        out_shape=[like((size, kv), BF16) for _, size in spans],
        scratch_shapes=[pltpu.VMEM((high - low, kv), F32), pltpu.SemaphoreType.DMA((len(cuts),))],
    )(weight, *deps)


def partial_grad(own, sib, cot, cot_sib, chip_step, spans, dtype, deps):
    kv = cot.shape[1]
    tokens = own.shape[0]
    rows = own.shape[1] // lax.axis_size("fsdp")

    def kernel(*refs):
        mine, theirs, cot_ref, cot_sib_ref = refs[:4]
        total = lax.dot_general(mine[...], cot_ref[...], OVER_ROWS, preferred_element_type=F32)
        total += lax.dot_general(theirs[...], cot_sib_ref[...], OVER_ROWS, preferred_element_type=F32)
        for (first, size, pad), out in zip(spans, refs[4 + len(deps) :]):
            out[:size, :] = total[first : first + size, :].astype(dtype)
            if pad:
                out[size:, :] = jnp.zeros((pad, kv), dtype)

    columns = pl.BlockSpec((tokens, rows), lambda g: (0, shard_at(chip_step, False)))
    whole = pl.BlockSpec((tokens, kv), lambda g: (0, 0))
    return call(
        kernel,
        "partial",
        grid=(1,),
        in_specs=[columns, columns, whole, whole] + [ANY] * len(deps),
        out_specs=[pl.BlockSpec((size + pad, kv), lambda g: (0, 0)) for _, size, pad in spans],
        out_shape=[like((size + pad, kv), dtype) for _, size, pad in spans],
    )(own, sib, cot, cot_sib, *deps)


def own_part(own, cot, chip_step):
    kv = cot.shape[1]
    tokens = own.shape[0]
    rows = own.shape[1] // lax.axis_size("fsdp")

    def kernel(mine, cot_ref, out):
        out[...] = lax.dot_general(mine[...], cot_ref[...], OVER_ROWS, preferred_element_type=F32)

    return call(
        kernel,
        "own_part",
        grid=(1,),
        in_specs=[
            pl.BlockSpec((tokens, rows), lambda g: (0, shard_at(chip_step, False))),
            pl.BlockSpec((tokens, kv), lambda g: (0, 0)),
        ],
        out_specs=VMEM,
        out_shape=pltpu.VMEM((rows, kv), F32),
    )(own, cot)


def add_part(begun, sib, cot_sib, chip_step, spans):
    kv = cot_sib.shape[1]
    tokens = sib.shape[0]
    rows = begun.shape[0]

    def kernel(begun_ref, theirs, cot_ref, *outs):
        total = lax.dot_general(theirs[...], cot_ref[...], OVER_ROWS, preferred_element_type=F32)
        for (first, size, _), out in zip(spans, outs):
            here = slice(first, first + size)
            out[...] = (begun_ref[here, :] + total[here, :]).astype(BF16)

    return call(
        kernel,
        "add_part",
        grid=(1,),
        in_specs=[
            VMEM,
            pl.BlockSpec((tokens, rows), lambda g: (0, shard_at(chip_step, False))),
            pl.BlockSpec((tokens, kv), lambda g: (0, 0)),
        ],
        out_specs=[VMEM] * len(spans),
        out_shape=[like((size, kv), BF16) for _, size, _ in spans],
    )(begun, sib, cot_sib)


def own_grad(own, sib, cot, cot_sib, held, step, deps):
    kv = cot.shape[1]
    tokens = own.shape[0]
    rows = own.shape[1] // lax.axis_size("fsdp")
    count = len(held)

    def kernel(*refs):
        step_ref, mine, theirs, cot_ref, cot_sib_ref = refs[:5]
        sources = refs[5 : 5 + count]
        out, scales, *places = refs[5 + count + len(deps) : -1]
        copies = [
            pltpu.make_async_copy(source, place, refs[-1].at[i])
            for i, (source, place) in enumerate(zip(sources, places))
        ]
        for copy in copies:
            copy.start()
        total = lax.dot_general(mine[...], cot_ref[...], OVER_ROWS, preferred_element_type=F32)
        total += lax.dot_general(theirs[...], cot_sib_ref[...], OVER_ROWS, preferred_element_type=F32)
        out[...] = total
        time = jnp.full((8, kv), (step_ref[0] + 1).astype(F32))
        for i, decay in enumerate((0.9, 0.95)):
            scales[8 * i : 8 * (i + 1), :] = 1.0 / (1.0 - jnp.exp(time * math.log(decay)))
        for copy in copies:
            copy.wait()

    columns = pl.BlockSpec((tokens, rows), lambda g: (0, shard_at(0, False)))
    whole = pl.BlockSpec((tokens, kv), lambda g: (0, 0))
    return call(
        kernel,
        "own_grad",
        grid=(1,),
        in_specs=[SMEM, columns, columns, whole, whole] + [ANY] * (count + len(deps)),
        out_specs=[VMEM] * (2 + count),
        out_shape=[pltpu.VMEM((rows, kv), F32), pltpu.VMEM((16, kv), F32)]
        + [pltpu.VMEM(array.shape, array.dtype) for array in held],
        scratch_shapes=[pltpu.SemaphoreType.DMA((count,))],
    )(step.reshape(1), own, sib, cot, cot_sib, *held, *deps)


def adam_rows(span, grad, got, weight, moments, scales, so_far, send, deps):
    first, size, pad = span
    rows, kv = weight.shape
    count = len(got)
    kept = 2 if send else 3
    strips = strips_of(size)

    def kernel(*refs):
        scales_ref, grad_ref = refs[:2]
        got_refs = refs[2 : 2 + count]
        w_ref, m_ref, v_ref = refs[2 + count : 5 + count]
        at = 5 + count + (kept if so_far else 0) + len(deps)
        places = refs[at : at + kept]
        at += kept
        if send:
            up_out, short_out = refs[at : at + 2]
            at += 2
        bufs, sems = refs[at : at + kept], refs[at + kept]
        copies = []
        scale1, scale2 = scales_ref[:1, :], scales_ref[8:9, :]
        for i, (strip, high) in enumerate(strips):
            here = slice(strip, strip + high)
            there = slice(first + strip, first + strip + high)
            g = grad_ref[there, :]
            for ref in got_refs:
                g += ref[here, :].astype(F32)
            w = w_ref[there, :]
            m = 0.9 * m_ref[there, :].astype(F32) + 0.1 * g
            v = 0.95 * v_ref[there, :].astype(F32) + 0.05 * g * g
            up = w - 0.003 * ((m * scale1) / (jnp.sqrt(v * scale2) + 1e-8) + 0.1 * w)
            bufs[0][here, :] = m.astype(BF16)
            bufs[1][here, :] = v.astype(BF16)
            if send:
                up_out[here, :] = up
                short_out[here, :] = up.astype(BF16)
            else:
                bufs[2][here, :] = up
            for j in range(kept):
                copies.append(
                    pltpu.make_async_copy(
                        bufs[j].at[pl.ds(strip, high), :],
                        places[j].at[0, pl.ds(first + strip, high), :],
                        sems.at[j, i],
                    )
                )
                copies[-1].start()
        if send and pad:
            short_out[size:, :] = jnp.zeros((pad, kv), BF16)
        for copy in copies:
            copy.wait()

    kinds = [BF16, BF16] + ([] if send else [F32])
    return call(
        kernel,
        "adam",
        in_specs=[VMEM] * (5 + count) + [HBM] * (kept if so_far else 0) + [ANY] * len(deps),
        out_specs=[HBM] * kept + ([VMEM, VMEM] if send else []),
        out_shape=[pltpu.HBM((1, rows, kv), kind) for kind in kinds]
        + ([like((size, kv), F32), like((size + pad, kv), BF16)] if send else []),
        scratch_shapes=[pltpu.VMEM((size, kv), kind) for kind in kinds]
        + [pltpu.SemaphoreType.DMA((kept, len(strips)))],
        input_output_aliases={5 + count + i: i for i in range(kept)} if so_far else {},
    )(scales, grad, *got, weight, *moments, *(so_far or ()), *deps)


def project(pieces, own, cot, so_far, last, deps, emit=()):
    tokens, width = own.shape
    kv = cot.shape[1]
    shard = width // lax.axis_size("fsdp")
    count = len(pieces)
    sizes = [piece[1] for piece in pieces]

    def kernel(*refs):
        weights, (cot_ref, own_ref) = refs[:count], refs[count : count + 2]
        at = count + 2
        if so_far:
            keys_ref = refs[at]
            at += 2
        at += len(deps)
        keys_out, back_out = refs[at : at + 2]
        spans_out = refs[at + 2 : at + 2 + len(emit)]
        at += 2 + len(emit)
        outs, shorts = refs[at : at + count], refs[at + count : at + count + len(emit)]
        keys_buf, sems = refs[-2:]
        stores = []
        for i, ((first, size), out) in enumerate(zip(emit, spans_out)):
            shorts[i][...] = weights[0][first : first + size, :].astype(BF16)
            stores.append(pltpu.make_async_copy(shorts[i], out, sems.at[count + 1 + i]))
            stores[-1].start()
        total = keys_ref[...] if so_far else None
        for j, (_, _, steps, other, first) in enumerate(pieces):
            place = pl.ds(pl.multiple_of(shard_at(steps, other) * shard + first, 128), sizes[j])
            rows = weights[j][: sizes[j], :].astype(BF16)
            outs[j][...] = lax.dot_general(
                cot_ref[...], rows, OVER_COLUMNS, preferred_element_type=F32
            ).astype(BF16)
            stores.append(pltpu.make_async_copy(outs[j], back_out.at[0, :, place], sems.at[j]))
            stores[-1].start()
            term = jnp.dot(own_ref[:, place], rows, preferred_element_type=F32)
            total = term if total is None else total + term
        if last:
            keys_buf[...] = total.astype(BF16)
            stores.append(pltpu.make_async_copy(keys_buf, keys_out.at[0], sems.at[count]))
            stores[-1].start()
        else:
            keys_out[...] = total
        for store in stores:
            store.wait()

    return call(
        kernel,
        "project",
        in_specs=[VMEM] * (count + 2) + ([VMEM, HBM] if so_far else []) + [ANY] * len(deps),
        out_specs=[HBM if last else VMEM, HBM] + [HBM] * len(emit),
        out_shape=[
            pltpu.HBM((1, tokens, kv), BF16) if last else like((tokens, kv), F32),
            pltpu.HBM((1, tokens, width), BF16),
        ]
        + [pltpu.HBM((size, kv), BF16) for _, size in emit],
        scratch_shapes=[pltpu.VMEM((tokens, size), BF16) for size in sizes]
        + [pltpu.VMEM((size, kv), BF16) for _, size in emit]
        + [pltpu.VMEM((tokens, kv), BF16), pltpu.SemaphoreType.DMA((count + 1 + len(emit),))],
        input_output_aliases={count + 3: 1} if so_far else {},
    )(*[piece[0] for piece in pieces], cot, own, *(so_far or ()), *deps)


def average(rows, spans, updated, neighbours, so_far, deps):
    kv = updated[0].shape[1]
    count = len(spans)
    strips = [(j, first, *strip) for j, (first, size, _) in enumerate(spans) for strip in strips_of(size)]

    def kernel(*refs):
        out, buf, sems = refs[-3:]
        copies = []
        for i, (j, first, strip, high) in enumerate(strips):
            here = slice(strip, strip + high)
            at = pl.ds(first - spans[0][0] + strip, high)
            buf[at, :] = 0.5 * (refs[j][here, :] + refs[count + j][here, :].astype(F32))
            copies.append(
                pltpu.make_async_copy(buf.at[at, :], out.at[0, pl.ds(first + strip, high), :], sems.at[i])
            )
            copies[-1].start()
        for copy in copies:
            copy.wait()

    before = [] if so_far is None else [so_far]
    return call(
        kernel,
        "average",
        in_specs=[VMEM] * (2 * count) + [HBM] * len(before) + [ANY] * len(deps),
        out_specs=HBM,
        out_shape=pltpu.HBM((1, rows, kv), F32),
        scratch_shapes=[
            pltpu.VMEM((sum(size for _, size, _ in spans), kv), F32),
            pltpu.SemaphoreType.DMA((len(strips),)),
        ],
        input_output_aliases={2 * count: 0} if before else {},
    )(*updated, *neighbours, *before, *deps)


def make_branch(distance):
    def branch(hidden, key_grad, weight, moment1, moment2, step):
        chips = lax.axis_size("fsdp") // CORES
        own, cot, w = hidden[0], key_grad[0], weight[0]
        state_in = (w, moment1[0], moment2[0])
        rows = w.shape[0]
        far = range(1, chips)

        def local_pieces(w_sib):
            return [(held[0], rows, 0, False, 0), (w_sib, rows, 0, True, 0)]

        def send_far(part, i):
            return [chip_shift(part, s, f"far{i}") for s in far]

        def pieces_of(i, arrays, order):
            first, size = w_spans[i]
            return [(v, size, s, False, first) for v, s in zip(arrays, far)] + [
                (core_swap(after(v, *order), f"swap{i}"), size, s, True, first) for v, s in zip(arrays, far)
            ]

        def adam(i, state, deps):
            return adam_rows(
                g_spans[i], grad, [got[s][i] for s in far], held[0], held[1:], scales, state, bool(distance), deps
            )

        def partial(s, spans, dtype, deps):
            return partial_grad(own, sib, cot, cot_sib, -s % chips, spans, dtype, deps)

        if 2 * distance >= lax.axis_size("rep"):
            g_spans = spans_of(rows, (20, 19, 25))
            w_spans = [span[:2] for span in spans_of(rows, (3, 3, 2))]
            sib, cot_sib = core_swap(own, "hidden"), core_swap(cot, "cot")
            sent = {s: add_part(own_part(own, cot, -s % chips), sib, cot_sib, -s % chips, g_spans) for s in far}
            got = {s: [chip_shift(part, s, f"grad{i}") for i, part in enumerate(sent[s])] for s in far}
            w_sib = core_swap(after(w, *[sent[s][-1] for s in far]), "w_sib")
            grad, scales, *held = own_grad(own, sib, cot, cot_sib, state_in, step, [sent[s][-1] for s in far])
            keys, back, *parts = project(local_pieces(w_sib), own, cot, None, False, [grad], w_spans)
            there = [send_far(part, i) for i, part in enumerate(parts)]
            state, order, updated, ups, near = None, keys, None, [], []
            for i in range(len(g_spans)):
                if i > 1:
                    updated = order = average(rows, [g_spans[i - 2]], [ups[i - 2]], [near[i - 2]], updated, [order])
                *state, up, order = adam(i, state, [order])
                ups.append(up)
                near.append(rep_shift(order, distance, f"near{i}"))
            updated = average(rows, [g_spans[-2]], [ups[-2]], [near[-2]], updated, [order])
            pieces = [piece for i in range(len(there)) for piece in pieces_of(i, there[i], [updated])]
            keys, back = project(pieces, own, cot, (keys, back), True, [updated])
            updated = average(rows, [g_spans[-1]], [ups[-1]], [near[-1]], updated, [keys])
        elif distance:
            g_spans = spans_of(rows, (25, 20, 19))
            w_spans = [span[:2] for span in spans_of(rows, (2, 3, 3))]
            sent_spans = [(w_spans[i][0], w_spans[i][1] + pad) for i, pad in enumerate((PAD, PAD, 0))]
            sib, cot_sib = core_swap(own, "hidden"), core_swap(cot, "cot")
            (w0,) = cast_rows(w, sent_spans[:1], [])
            there = [send_far(w0, 0)]
            sent = {s: partial(s, g_spans, BF16, [w0]) for s in far}
            got = {s: [chip_shift(part, s, f"grad{i}") for i, part in enumerate(sent[s])] for s in far}
            w_sib = core_swap(after(w, w0), "w_sib")
            grad, scales, *held = own_grad(own, sib, cot, cot_sib, state_in, step, [sent[s][-1] for s in far])
            pieces = local_pieces(w_sib) + pieces_of(0, there[0], [grad])
            keys, back, *parts = project(pieces, own, cot, None, False, [grad], sent_spans[1:])
            there += [send_far(part, 1 + i) for i, part in enumerate(parts)]
            state, order, ups, near = None, keys, [], []
            for i in range(len(g_spans)):
                *state, up, order = adam(i, state, [order])
                ups.append(up)
                near.append(rep_shift(order, distance, f"near{i}"))
            updated = average(rows, g_spans, ups, near, None, [order])
            pieces = pieces_of(1, there[1], [order]) + pieces_of(2, there[2], [updated])
            last = len(far)
            keys, back = project(pieces[:-last], own, cot, (keys, back), False, [updated])
            keys, back = project(pieces[-last:], own, cot, (keys, back), True, [])
        else:
            g_spans = spans_of(rows, (13, 3))
            w_spans = [span[:2] for span in spans_of(rows, (1, 1))]
            sib, cot_sib, w_sib = core_swap(own, "hidden"), core_swap(cot, "cot"), core_swap(w, "w_sib")
            parts = cast_rows(w, w_spans, [])
            there = [send_far(part, i) for i, part in enumerate(parts)]
            sent = {s: partial(s, g_spans, BF16, [parts[0]]) for s in far}
            got = {s: [chip_shift(part, s, f"grad{i}") for i, part in enumerate(sent[s])] for s in far}
            grad, scales, *held = own_grad(own, sib, cot, cot_sib, state_in, step, [sent[s][-1] for s in far])
            keys, back = project(local_pieces(w_sib), own, cot, None, False, [grad])
            pieces = [piece for i in range(len(there)) for piece in pieces_of(i, there[i], [keys])]
            keys, back = project(pieces, own, cot, (keys, back), True, [keys])
            state = adam(0, None, [keys])
            state = adam(1, state, [])
            updated = state[2]
        return keys, back, updated, state[0], state[1]

    return branch


def per_device(hidden, key_grad, weight, moment1, moment2, step):
    replicas = lax.axis_size("rep")
    distances = [2**level % replicas for level in range(LEVELS)]
    kinds = sorted(set(distances))
    level = lax.rem(step, LEVELS)
    pick = jnp.int32(0)
    for i, d in enumerate(distances):
        pick = jnp.where(level == i, kinds.index(d), pick)
    return lax.switch(
        pick, [make_branch(d) for d in kinds], hidden, key_grad, weight, moment1, moment2, step
    )


def solution(mesh):
    spec = P("rep", "fsdp", None)
    return jax.shard_map(
        per_device,
        mesh=mesh,
        in_specs=(spec,) * 5 + (P(),),
        out_specs=(spec,) * 5,
        check_vma=False,
    )
```

```python
import math

import jax
import jax.numpy as jnp
from jax import lax
from jax.experimental import pallas as pl
from jax.experimental.pallas import tpu as pltpu
from jax.sharding import PartitionSpec as P

LEVELS = 6
CORES = 2
PAD = 16
STRIP = 128
F32 = jnp.float32
BF16 = jnp.bfloat16
ANY = pl.BlockSpec(memory_space=pl.ANY)
HBM = pl.BlockSpec(memory_space=pltpu.HBM)
SMEM = pl.BlockSpec(memory_space=pltpu.SMEM)
VMEM = pl.BlockSpec(memory_space=pltpu.VMEM)
PARAMS = pltpu.CompilerParams(vmem_limit_bytes=16 * 2**20)
OVER_ROWS = (((0,), (0,)), ((), ()))
OVER_COLUMNS = (((1,), (1,)), ((), ()))


def call(kernel, name, **kwargs):
    with jax.named_scope(name):
        return pl.pallas_call(kernel, name=name, compiler_params=PARAMS, **kwargs)


def like(shape, dtype):
    return jax.ShapeDtypeStruct(shape, dtype)


def core_swap(value, name):
    n = lax.axis_size("fsdp")
    with jax.named_scope(name):
        return lax.ppermute(value, "fsdp", [(i, i ^ 1) for i in range(n)])


def chip_shift(value, distance, name):
    n = lax.axis_size("fsdp")
    with jax.named_scope(name):
        return lax.ppermute(value, "fsdp", [(i, (i + CORES * distance) % n) for i in range(n)])


def rep_shift(value, distance, name):
    n = lax.axis_size("rep")
    with jax.named_scope(name):
        return lax.ppermute(value, "rep", [((i - distance) % n, i) for i in range(n)])


def after(value, *done):
    return lax.optimization_barrier((value, *done))[0]


def shard_at(chip_step, other_core):
    n = lax.axis_size("fsdp")
    me = lax.axis_index("fsdp")
    core = lax.rem(me, CORES)
    if other_core:
        core = 1 - core
    return lax.rem(lax.div(me, CORES) + n // CORES - chip_step, n // CORES) * CORES + core


def spans_of(rows, shares, pads=None):
    unit = rows // sum(shares)
    pads = pads or (0,) * len(shares)
    return [(sum(shares[:i]) * unit, share * unit, pads[i]) for i, share in enumerate(shares)]


def strips_of(size):
    return [(at, min(STRIP, size - at)) for at in range(0, size, STRIP)]


def cast_rows(weight, spans, deps):
    kv = weight.shape[1]
    low, high = spans[0][0], sum(spans[-1])

    cuts = [(first + at, high) for first, size in spans for at, high in strips_of(size)]

    def kernel(src, *refs):
        buf, sems = refs[-2:]
        loads = [
            pltpu.make_async_copy(
                src.at[pl.ds(at, high), :], buf.at[pl.ds(at - low, high), :], sems.at[i]
            )
            for i, (at, high) in enumerate(cuts)
        ]
        for load in loads:
            load.start()
        loads = iter(loads)
        for (first, size), out in zip(spans, refs[len(deps) :]):
            for at, high in strips_of(size):
                next(loads).wait()
                here = first - low + at
                out[at : at + high, :] = buf[here : here + high, :].astype(BF16)

    return call(
        kernel,
        "cast",
        in_specs=[ANY] * (1 + len(deps)),
        out_specs=[VMEM] * len(spans),
        out_shape=[like((size, kv), BF16) for _, size in spans],
        scratch_shapes=[pltpu.VMEM((high - low, kv), F32), pltpu.SemaphoreType.DMA((len(cuts),))],
    )(weight, *deps)


def partial_grad(own, sib, cot, cot_sib, chip_step, spans, dtype, deps):
    kv = cot.shape[1]
    tokens = own.shape[0]
    rows = own.shape[1] // lax.axis_size("fsdp")

    def kernel(*refs):
        mine, theirs, cot_ref, cot_sib_ref = refs[:4]
        total = lax.dot_general(mine[...], cot_ref[...], OVER_ROWS, preferred_element_type=F32)
        total += lax.dot_general(theirs[...], cot_sib_ref[...], OVER_ROWS, preferred_element_type=F32)
        for (first, size, pad), out in zip(spans, refs[4 + len(deps) :]):
            out[:size, :] = total[first : first + size, :].astype(dtype)
            if pad:
                out[size:, :] = jnp.zeros((pad, kv), dtype)

    columns = pl.BlockSpec((tokens, rows), lambda g: (0, shard_at(chip_step, False)))
    whole = pl.BlockSpec((tokens, kv), lambda g: (0, 0))
    return call(
        kernel,
        "partial",
        grid=(1,),
        in_specs=[columns, columns, whole, whole] + [ANY] * len(deps),
        out_specs=[pl.BlockSpec((size + pad, kv), lambda g: (0, 0)) for _, size, pad in spans],
        out_shape=[like((size + pad, kv), dtype) for _, size, pad in spans],
    )(own, sib, cot, cot_sib, *deps)


def own_part(own, cot, chip_step):
    kv = cot.shape[1]
    tokens = own.shape[0]
    rows = own.shape[1] // lax.axis_size("fsdp")

    def kernel(mine, cot_ref, out):
        out[...] = lax.dot_general(mine[...], cot_ref[...], OVER_ROWS, preferred_element_type=F32)

    return call(
        kernel,
        "own_part",
        grid=(1,),
        in_specs=[
            pl.BlockSpec((tokens, rows), lambda g: (0, shard_at(chip_step, False))),
            pl.BlockSpec((tokens, kv), lambda g: (0, 0)),
        ],
        out_specs=VMEM,
        out_shape=pltpu.VMEM((rows, kv), F32),
    )(own, cot)


def add_part(begun, sib, cot_sib, chip_step, spans):
    kv = cot_sib.shape[1]
    tokens = sib.shape[0]
    rows = begun.shape[0]

    def kernel(begun_ref, theirs, cot_ref, *outs):
        total = lax.dot_general(theirs[...], cot_ref[...], OVER_ROWS, preferred_element_type=F32)
        for (first, size, _), out in zip(spans, outs):
            here = slice(first, first + size)
            out[...] = (begun_ref[here, :] + total[here, :]).astype(BF16)

    return call(
        kernel,
        "add_part",
        grid=(1,),
        in_specs=[
            VMEM,
            pl.BlockSpec((tokens, rows), lambda g: (0, shard_at(chip_step, False))),
            pl.BlockSpec((tokens, kv), lambda g: (0, 0)),
        ],
        out_specs=[VMEM] * len(spans),
        out_shape=[like((size, kv), BF16) for _, size, _ in spans],
    )(begun, sib, cot_sib)


def own_grad(own, sib, cot, cot_sib, held, step, deps):
    kv = cot.shape[1]
    tokens = own.shape[0]
    rows = own.shape[1] // lax.axis_size("fsdp")
    count = len(held)

    def kernel(*refs):
        step_ref, mine, theirs, cot_ref, cot_sib_ref = refs[:5]
        sources = refs[5 : 5 + count]
        out, scales, *places = refs[5 + count + len(deps) : -1]
        copies = [
            pltpu.make_async_copy(source, place, refs[-1].at[i])
            for i, (source, place) in enumerate(zip(sources, places))
        ]
        for copy in copies:
            copy.start()
        total = lax.dot_general(mine[...], cot_ref[...], OVER_ROWS, preferred_element_type=F32)
        total += lax.dot_general(theirs[...], cot_sib_ref[...], OVER_ROWS, preferred_element_type=F32)
        out[...] = total
        time = jnp.full((8, kv), (step_ref[0] + 1).astype(F32))
        for i, decay in enumerate((0.9, 0.95)):
            scales[8 * i : 8 * (i + 1), :] = 1.0 / (1.0 - jnp.exp(time * math.log(decay)))
        for copy in copies:
            copy.wait()

    columns = pl.BlockSpec((tokens, rows), lambda g: (0, shard_at(0, False)))
    whole = pl.BlockSpec((tokens, kv), lambda g: (0, 0))
    return call(
        kernel,
        "own_grad",
        grid=(1,),
        in_specs=[SMEM, columns, columns, whole, whole] + [ANY] * (count + len(deps)),
        out_specs=[VMEM] * (2 + count),
        out_shape=[pltpu.VMEM((rows, kv), F32), pltpu.VMEM((16, kv), F32)]
        + [pltpu.VMEM(array.shape, array.dtype) for array in held],
        scratch_shapes=[pltpu.SemaphoreType.DMA((count,))],
    )(step.reshape(1), own, sib, cot, cot_sib, *held, *deps)


def adam_rows(span, grad, got, weight, moments, scales, so_far, send, deps):
    first, size, pad = span
    rows, kv = weight.shape
    count = len(got)
    kept = 2 if send else 3
    strips = strips_of(size)

    def kernel(*refs):
        scales_ref, grad_ref = refs[:2]
        got_refs = refs[2 : 2 + count]
        w_ref, m_ref, v_ref = refs[2 + count : 5 + count]
        at = 5 + count + (kept if so_far else 0) + len(deps)
        places = refs[at : at + kept]
        at += kept
        if send:
            up_out, short_out = refs[at : at + 2]
            at += 2
        bufs, sems = refs[at : at + kept], refs[at + kept]
        copies = []
        scale1, scale2 = scales_ref[:1, :], scales_ref[8:9, :]
        for i, (strip, high) in enumerate(strips):
            here = slice(strip, strip + high)
            there = slice(first + strip, first + strip + high)
            g = grad_ref[there, :]
            for ref in got_refs:
                g += ref[here, :].astype(F32)
            w = w_ref[there, :]
            m = 0.9 * m_ref[there, :].astype(F32) + 0.1 * g
            v = 0.95 * v_ref[there, :].astype(F32) + 0.05 * g * g
            up = w - 0.003 * ((m * scale1) / (jnp.sqrt(v * scale2) + 1e-8) + 0.1 * w)
            bufs[0][here, :] = m.astype(BF16)
            bufs[1][here, :] = v.astype(BF16)
            if send:
                up_out[here, :] = up
                short_out[here, :] = up.astype(BF16)
            else:
                bufs[2][here, :] = up
            for j in range(kept):
                copies.append(
                    pltpu.make_async_copy(
                        bufs[j].at[pl.ds(strip, high), :],
                        places[j].at[0, pl.ds(first + strip, high), :],
                        sems.at[j, i],
                    )
                )
                copies[-1].start()
        if send and pad:
            short_out[size:, :] = jnp.zeros((pad, kv), BF16)
        for copy in copies:
            copy.wait()

    kinds = [BF16, BF16] + ([] if send else [F32])
    return call(
        kernel,
        "adam",
        in_specs=[VMEM] * (5 + count) + [HBM] * (kept if so_far else 0) + [ANY] * len(deps),
        out_specs=[HBM] * kept + ([VMEM, VMEM] if send else []),
        out_shape=[pltpu.HBM((1, rows, kv), kind) for kind in kinds]
        + ([like((size, kv), F32), like((size + pad, kv), BF16)] if send else []),
        scratch_shapes=[pltpu.VMEM((size, kv), kind) for kind in kinds]
        + [pltpu.SemaphoreType.DMA((kept, len(strips)))],
        input_output_aliases={5 + count + i: i for i in range(kept)} if so_far else {},
    )(scales, grad, *got, weight, *moments, *(so_far or ()), *deps)


def project(pieces, own, cot, so_far, last, deps, emit=()):
    tokens, width = own.shape
    kv = cot.shape[1]
    shard = width // lax.axis_size("fsdp")
    count = len(pieces)
    sizes = [piece[1] for piece in pieces]

    def kernel(*refs):
        weights, (cot_ref, own_ref) = refs[:count], refs[count : count + 2]
        at = count + 2
        if so_far:
            keys_ref = refs[at]
            at += 2
        at += len(deps)
        keys_out, back_out = refs[at : at + 2]
        spans_out = refs[at + 2 : at + 2 + len(emit)]
        at += 2 + len(emit)
        outs, shorts = refs[at : at + count], refs[at + count : at + count + len(emit)]
        keys_buf, sems = refs[-2:]
        stores = []
        for i, ((first, size), out) in enumerate(zip(emit, spans_out)):
            shorts[i][...] = weights[0][first : first + size, :].astype(BF16)
            stores.append(pltpu.make_async_copy(shorts[i], out, sems.at[count + 1 + i]))
            stores[-1].start()
        total = keys_ref[...] if so_far else None
        for j, (_, _, steps, other, first) in enumerate(pieces):
            place = pl.ds(pl.multiple_of(shard_at(steps, other) * shard + first, 128), sizes[j])
            rows = weights[j][: sizes[j], :].astype(BF16)
            outs[j][...] = lax.dot_general(
                cot_ref[...], rows, OVER_COLUMNS, preferred_element_type=F32
            ).astype(BF16)
            stores.append(pltpu.make_async_copy(outs[j], back_out.at[0, :, place], sems.at[j]))
            stores[-1].start()
            term = jnp.dot(own_ref[:, place], rows, preferred_element_type=F32)
            total = term if total is None else total + term
        if last:
            keys_buf[...] = total.astype(BF16)
            stores.append(pltpu.make_async_copy(keys_buf, keys_out.at[0], sems.at[count]))
            stores[-1].start()
        else:
            keys_out[...] = total
        for store in stores:
            store.wait()

    return call(
        kernel,
        "project",
        in_specs=[VMEM] * (count + 2) + ([VMEM, HBM] if so_far else []) + [ANY] * len(deps),
        out_specs=[HBM if last else VMEM, HBM] + [HBM] * len(emit),
        out_shape=[
            pltpu.HBM((1, tokens, kv), BF16) if last else like((tokens, kv), F32),
            pltpu.HBM((1, tokens, width), BF16),
        ]
        + [pltpu.HBM((size, kv), BF16) for _, size in emit],
        scratch_shapes=[pltpu.VMEM((tokens, size), BF16) for size in sizes]
        + [pltpu.VMEM((size, kv), BF16) for _, size in emit]
        + [pltpu.VMEM((tokens, kv), BF16), pltpu.SemaphoreType.DMA((count + 1 + len(emit),))],
        input_output_aliases={count + 3: 1} if so_far else {},
    )(*[piece[0] for piece in pieces], cot, own, *(so_far or ()), *deps)


def average(rows, spans, updated, neighbours, so_far, deps):
    kv = updated[0].shape[1]
    count = len(spans)
    strips = [(j, first, *strip) for j, (first, size, _) in enumerate(spans) for strip in strips_of(size)]

    def kernel(*refs):
        out, buf, sems = refs[-3:]
        copies = []
        for i, (j, first, strip, high) in enumerate(strips):
            here = slice(strip, strip + high)
            at = pl.ds(first - spans[0][0] + strip, high)
            buf[at, :] = 0.5 * (refs[j][here, :] + refs[count + j][here, :].astype(F32))
            copies.append(
                pltpu.make_async_copy(buf.at[at, :], out.at[0, pl.ds(first + strip, high), :], sems.at[i])
            )
            copies[-1].start()
        for copy in copies:
            copy.wait()

    before = [] if so_far is None else [so_far]
    return call(
        kernel,
        "average",
        in_specs=[VMEM] * (2 * count) + [HBM] * len(before) + [ANY] * len(deps),
        out_specs=HBM,
        out_shape=pltpu.HBM((1, rows, kv), F32),
        scratch_shapes=[
            pltpu.VMEM((sum(size for _, size, _ in spans), kv), F32),
            pltpu.SemaphoreType.DMA((len(strips),)),
        ],
        input_output_aliases={2 * count: 0} if before else {},
    )(*updated, *neighbours, *before, *deps)


def make_branch(distance):
    def branch(hidden, key_grad, weight, moment1, moment2, step):
        chips = lax.axis_size("fsdp") // CORES
        own, cot, w = hidden[0], key_grad[0], weight[0]
        state_in = (w, moment1[0], moment2[0])
        rows = w.shape[0]
        far = range(1, chips)

        def local_pieces(w_sib):
            return [(held[0], rows, 0, False, 0), (w_sib, rows, 0, True, 0)]

        def send_far(part, i):
            return [chip_shift(part, s, f"far{i}") for s in far]

        def pieces_of(i, arrays, order):
            first, size = w_spans[i]
            return [(v, size, s, False, first) for v, s in zip(arrays, far)] + [
                (core_swap(after(v, *order), f"swap{i}"), size, s, True, first) for v, s in zip(arrays, far)
            ]

        def adam(i, state, deps):
            return adam_rows(
                g_spans[i], grad, [got[s][i] for s in far], held[0], held[1:], scales, state, bool(distance), deps
            )

        def partial(s, spans, dtype, deps):
            return partial_grad(own, sib, cot, cot_sib, -s % chips, spans, dtype, deps)

        if 2 * distance >= lax.axis_size("rep"):
            g_spans = spans_of(rows, (20, 19, 25))
            w_spans = [span[:2] for span in spans_of(rows, (3, 3, 2))]
            sib, cot_sib = core_swap(own, "hidden"), core_swap(cot, "cot")
            sent = {s: add_part(own_part(own, cot, -s % chips), sib, cot_sib, -s % chips, g_spans) for s in far}
            got = {s: [chip_shift(part, s, f"grad{i}") for i, part in enumerate(sent[s])] for s in far}
            w_sib = core_swap(after(w, *[sent[s][-1] for s in far]), "w_sib")
            grad, scales, *held = own_grad(own, sib, cot, cot_sib, state_in, step, [sent[s][-1] for s in far])
            keys, back, *parts = project(local_pieces(w_sib), own, cot, None, False, [grad], w_spans)
            there = [send_far(part, i) for i, part in enumerate(parts)]
            state, order, updated, ups, near = None, keys, None, [], []
            for i in range(len(g_spans)):
                if i > 1:
                    updated = order = average(rows, [g_spans[i - 2]], [ups[i - 2]], [near[i - 2]], updated, [order])
                *state, up, order = adam(i, state, [order])
                ups.append(up)
                near.append(rep_shift(order, distance, f"near{i}"))
            updated = average(rows, [g_spans[-2]], [ups[-2]], [near[-2]], updated, [order])
            pieces = [piece for i in range(len(there)) for piece in pieces_of(i, there[i], [updated])]
            keys, back = project(pieces, own, cot, (keys, back), True, [updated])
            updated = average(rows, [g_spans[-1]], [ups[-1]], [near[-1]], updated, [keys])
        elif distance:
            g_spans = spans_of(rows, (25, 20, 19))
            w_spans = [span[:2] for span in spans_of(rows, (2, 3, 3))]
            sent_spans = [(w_spans[i][0], w_spans[i][1] + pad) for i, pad in enumerate((PAD, PAD, 0))]
            sib, cot_sib = core_swap(own, "hidden"), core_swap(cot, "cot")
            (w0,) = cast_rows(w, sent_spans[:1], [])
            there = [send_far(w0, 0)]
            sent = {s: partial(s, g_spans, BF16, [w0]) for s in far}
            got = {s: [chip_shift(part, s, f"grad{i}") for i, part in enumerate(sent[s])] for s in far}
            w_sib = core_swap(after(w, w0), "w_sib")
            grad, scales, *held = own_grad(own, sib, cot, cot_sib, state_in, step, [sent[s][-1] for s in far])
            pieces = local_pieces(w_sib) + pieces_of(0, there[0], [grad])
            keys, back, *parts = project(pieces, own, cot, None, False, [grad], sent_spans[1:])
            there += [send_far(part, 1 + i) for i, part in enumerate(parts)]
            state, order, ups, near = None, keys, [], []
            for i in range(len(g_spans)):
                *state, up, order = adam(i, state, [order])
                ups.append(up)
                near.append(rep_shift(order, distance, f"near{i}"))
            updated = average(rows, g_spans, ups, near, None, [order])
            pieces = pieces_of(1, there[1], [order]) + pieces_of(2, there[2], [updated])
            last = len(far)
            keys, back = project(pieces[:-last], own, cot, (keys, back), False, [updated])
            keys, back = project(pieces[-last:], own, cot, (keys, back), True, [])
        else:
            g_spans = spans_of(rows, (47, 17))
            w_spans = [span[:2] for span in spans_of(rows, (1, 1))]
            sib, w_sib = core_swap(own, "hidden"), core_swap(w, "w_sib")
            parts = cast_rows(w, w_spans, [])
            cot_sib = core_swap(after(cot, parts[0]), "cot")
            there = [send_far(part, i) for i, part in enumerate(parts)]
            sent = {s: partial(s, g_spans, BF16, [parts[0]]) for s in far}
            got = {s: [chip_shift(part, s, f"grad{i}") for i, part in enumerate(sent[s])] for s in far}
            grad, scales, *held = own_grad(own, sib, cot, cot_sib, state_in, step, [sent[s][-1] for s in far])
            keys, back = project(local_pieces(w_sib), own, cot, None, False, [grad])
            pieces = [piece for i in range(len(there)) for piece in pieces_of(i, there[i], [keys])]
            keys, back = project(pieces, own, cot, (keys, back), True, [keys])
            state = adam(0, None, [keys])
            state = adam(1, state, [])
            updated = state[2]
        return keys, back, updated, state[0], state[1]

    return branch


def per_device(hidden, key_grad, weight, moment1, moment2, step):
    replicas = lax.axis_size("rep")
    distances = [2**level % replicas for level in range(LEVELS)]
    kinds = sorted(set(distances))
    level = lax.rem(step, LEVELS)
    pick = jnp.int32(0)
    for i, d in enumerate(distances):
        pick = jnp.where(level == i, kinds.index(d), pick)
    return lax.switch(
        pick, [make_branch(d) for d in kinds], hidden, key_grad, weight, moment1, moment2, step
    )


def solution(mesh):
    spec = P("rep", "fsdp", None)
    return jax.shard_map(
        per_device,
        mesh=mesh,
        in_specs=(spec,) * 5 + (P(),),
        out_specs=(spec,) * 5,
        check_vma=False,
    )
```

```python
import math

import jax
import jax.numpy as jnp
from jax import lax
from jax.experimental import pallas as pl
from jax.experimental.pallas import tpu as pltpu
from jax.sharding import PartitionSpec as P

LEVELS = 6
CORES = 2
PAD = 16
STRIP = 128
F32 = jnp.float32
BF16 = jnp.bfloat16
ANY = pl.BlockSpec(memory_space=pl.ANY)
HBM = pl.BlockSpec(memory_space=pltpu.HBM)
SMEM = pl.BlockSpec(memory_space=pltpu.SMEM)
VMEM = pl.BlockSpec(memory_space=pltpu.VMEM)
PARAMS = pltpu.CompilerParams(vmem_limit_bytes=16 * 2**20)
OVER_ROWS = (((0,), (0,)), ((), ()))
OVER_COLUMNS = (((1,), (1,)), ((), ()))


def call(kernel, name, **kwargs):
    with jax.named_scope(name):
        return pl.pallas_call(kernel, name=name, compiler_params=PARAMS, **kwargs)


def like(shape, dtype):
    return jax.ShapeDtypeStruct(shape, dtype)


def core_swap(value, name):
    n = lax.axis_size("fsdp")
    with jax.named_scope(name):
        return lax.ppermute(value, "fsdp", [(i, i ^ 1) for i in range(n)])


def chip_shift(value, distance, name):
    n = lax.axis_size("fsdp")
    with jax.named_scope(name):
        return lax.ppermute(value, "fsdp", [(i, (i + CORES * distance) % n) for i in range(n)])


def rep_shift(value, distance, name):
    n = lax.axis_size("rep")
    with jax.named_scope(name):
        return lax.ppermute(value, "rep", [((i - distance) % n, i) for i in range(n)])


def after(value, *done):
    return lax.optimization_barrier((value, *done))[0]


def shard_at(chip_step, other_core):
    n = lax.axis_size("fsdp")
    me = lax.axis_index("fsdp")
    core = lax.rem(me, CORES)
    if other_core:
        core = 1 - core
    return lax.rem(lax.div(me, CORES) + n // CORES - chip_step, n // CORES) * CORES + core


def spans_of(rows, shares, pads=None):
    unit = rows // sum(shares)
    pads = pads or (0,) * len(shares)
    return [(sum(shares[:i]) * unit, share * unit, pads[i]) for i, share in enumerate(shares)]


def strips_of(size):
    return [(at, min(STRIP, size - at)) for at in range(0, size, STRIP)]


def cast_rows(weight, spans, deps):
    kv = weight.shape[1]
    low, high = spans[0][0], sum(spans[-1])

    cuts = [(first + at, high) for first, size in spans for at, high in strips_of(size)]

    def kernel(src, *refs):
        buf, sems = refs[-2:]
        loads = [
            pltpu.make_async_copy(
                src.at[pl.ds(at, high), :], buf.at[pl.ds(at - low, high), :], sems.at[i]
            )
            for i, (at, high) in enumerate(cuts)
        ]
        for load in loads:
            load.start()
        loads = iter(loads)
        for (first, size), out in zip(spans, refs[len(deps) :]):
            for at, high in strips_of(size):
                next(loads).wait()
                here = first - low + at
                out[at : at + high, :] = buf[here : here + high, :].astype(BF16)

    return call(
        kernel,
        "cast",
        in_specs=[ANY] * (1 + len(deps)),
        out_specs=[VMEM] * len(spans),
        out_shape=[like((size, kv), BF16) for _, size in spans],
        scratch_shapes=[pltpu.VMEM((high - low, kv), F32), pltpu.SemaphoreType.DMA((len(cuts),))],
    )(weight, *deps)


def partial_grad(own, sib, cot, cot_sib, chip_step, spans, dtype, deps):
    kv = cot.shape[1]
    tokens = own.shape[0]
    rows = own.shape[1] // lax.axis_size("fsdp")

    def kernel(*refs):
        mine, theirs, cot_ref, cot_sib_ref = refs[:4]
        total = lax.dot_general(mine[...], cot_ref[...], OVER_ROWS, preferred_element_type=F32)
        total += lax.dot_general(theirs[...], cot_sib_ref[...], OVER_ROWS, preferred_element_type=F32)
        for (first, size, pad), out in zip(spans, refs[4 + len(deps) :]):
            out[:size, :] = total[first : first + size, :].astype(dtype)
            if pad:
                out[size:, :] = jnp.zeros((pad, kv), dtype)

    columns = pl.BlockSpec((tokens, rows), lambda g: (0, shard_at(chip_step, False)))
    whole = pl.BlockSpec((tokens, kv), lambda g: (0, 0))
    return call(
        kernel,
        "partial",
        grid=(1,),
        in_specs=[columns, columns, whole, whole] + [ANY] * len(deps),
        out_specs=[pl.BlockSpec((size + pad, kv), lambda g: (0, 0)) for _, size, pad in spans],
        out_shape=[like((size + pad, kv), dtype) for _, size, pad in spans],
    )(own, sib, cot, cot_sib, *deps)


def own_part(own, cot, chip_step):
    kv = cot.shape[1]
    tokens = own.shape[0]
    rows = own.shape[1] // lax.axis_size("fsdp")

    def kernel(mine, cot_ref, out):
        out[...] = lax.dot_general(mine[...], cot_ref[...], OVER_ROWS, preferred_element_type=F32)

    return call(
        kernel,
        "own_part",
        grid=(1,),
        in_specs=[
            pl.BlockSpec((tokens, rows), lambda g: (0, shard_at(chip_step, False))),
            pl.BlockSpec((tokens, kv), lambda g: (0, 0)),
        ],
        out_specs=VMEM,
        out_shape=pltpu.VMEM((rows, kv), F32),
    )(own, cot)


def add_part(begun, sib, cot_sib, chip_step, spans):
    kv = cot_sib.shape[1]
    tokens = sib.shape[0]
    rows = begun.shape[0]

    def kernel(begun_ref, theirs, cot_ref, *outs):
        total = lax.dot_general(theirs[...], cot_ref[...], OVER_ROWS, preferred_element_type=F32)
        for (first, size, _), out in zip(spans, outs):
            here = slice(first, first + size)
            out[...] = (begun_ref[here, :] + total[here, :]).astype(BF16)

    return call(
        kernel,
        "add_part",
        grid=(1,),
        in_specs=[
            VMEM,
            pl.BlockSpec((tokens, rows), lambda g: (0, shard_at(chip_step, False))),
            pl.BlockSpec((tokens, kv), lambda g: (0, 0)),
        ],
        out_specs=[VMEM] * len(spans),
        out_shape=[like((size, kv), BF16) for _, size, _ in spans],
    )(begun, sib, cot_sib)


def own_grad(own, sib, cot, cot_sib, held, step, deps):
    kv = cot.shape[1]
    tokens = own.shape[0]
    rows = own.shape[1] // lax.axis_size("fsdp")
    count = len(held)

    def kernel(*refs):
        step_ref, mine, theirs, cot_ref, cot_sib_ref = refs[:5]
        sources = refs[5 : 5 + count]
        out, scales, *places = refs[5 + count + len(deps) : -1]
        copies = [
            pltpu.make_async_copy(source, place, refs[-1].at[i])
            for i, (source, place) in enumerate(zip(sources, places))
        ]
        for copy in copies:
            copy.start()
        total = lax.dot_general(mine[...], cot_ref[...], OVER_ROWS, preferred_element_type=F32)
        total += lax.dot_general(theirs[...], cot_sib_ref[...], OVER_ROWS, preferred_element_type=F32)
        out[...] = total
        time = jnp.full((8, kv), (step_ref[0] + 1).astype(F32))
        for i, decay in enumerate((0.9, 0.95)):
            scales[8 * i : 8 * (i + 1), :] = 1.0 / (1.0 - jnp.exp(time * math.log(decay)))
        for copy in copies:
            copy.wait()

    columns = pl.BlockSpec((tokens, rows), lambda g: (0, shard_at(0, False)))
    whole = pl.BlockSpec((tokens, kv), lambda g: (0, 0))
    return call(
        kernel,
        "own_grad",
        grid=(1,),
        in_specs=[SMEM, columns, columns, whole, whole] + [ANY] * (count + len(deps)),
        out_specs=[VMEM] * (2 + count),
        out_shape=[pltpu.VMEM((rows, kv), F32), pltpu.VMEM((16, kv), F32)]
        + [pltpu.VMEM(array.shape, array.dtype) for array in held],
        scratch_shapes=[pltpu.SemaphoreType.DMA((count,))],
    )(step.reshape(1), own, sib, cot, cot_sib, *held, *deps)


def adam_rows(span, grad, got, weight, moments, scales, so_far, send, deps):
    first, size, pad = span
    rows, kv = weight.shape
    count = len(got)
    kept = 2 if send else 3
    strips = strips_of(size)

    def kernel(*refs):
        scales_ref, grad_ref = refs[:2]
        got_refs = refs[2 : 2 + count]
        w_ref, m_ref, v_ref = refs[2 + count : 5 + count]
        at = 5 + count + (kept if so_far else 0) + len(deps)
        places = refs[at : at + kept]
        at += kept
        if send:
            up_out, short_out = refs[at : at + 2]
            at += 2
        bufs, sems = refs[at : at + kept], refs[at + kept]
        copies = []
        scale1, scale2 = scales_ref[:1, :], scales_ref[8:9, :]
        for i, (strip, high) in enumerate(strips):
            here = slice(strip, strip + high)
            there = slice(first + strip, first + strip + high)
            g = grad_ref[there, :]
            for ref in got_refs:
                g += ref[here, :].astype(F32)
            w = w_ref[there, :]
            m = 0.9 * m_ref[there, :].astype(F32) + 0.1 * g
            v = 0.95 * v_ref[there, :].astype(F32) + 0.05 * g * g
            up = w - 0.003 * ((m * scale1) / (jnp.sqrt(v * scale2) + 1e-8) + 0.1 * w)
            bufs[0][here, :] = m.astype(BF16)
            bufs[1][here, :] = v.astype(BF16)
            if send:
                up_out[here, :] = up
                short_out[here, :] = up.astype(BF16)
            else:
                bufs[2][here, :] = up
            for j in range(kept):
                copies.append(
                    pltpu.make_async_copy(
                        bufs[j].at[pl.ds(strip, high), :],
                        places[j].at[0, pl.ds(first + strip, high), :],
                        sems.at[j, i],
                    )
                )
                copies[-1].start()
        if send and pad:
            short_out[size:, :] = jnp.zeros((pad, kv), BF16)
        for copy in copies:
            copy.wait()

    kinds = [BF16, BF16] + ([] if send else [F32])
    return call(
        kernel,
        "adam",
        in_specs=[VMEM] * (5 + count) + [HBM] * (kept if so_far else 0) + [ANY] * len(deps),
        out_specs=[HBM] * kept + ([VMEM, VMEM] if send else []),
        out_shape=[pltpu.HBM((1, rows, kv), kind) for kind in kinds]
        + ([like((size, kv), F32), like((size + pad, kv), BF16)] if send else []),
        scratch_shapes=[pltpu.VMEM((size, kv), kind) for kind in kinds]
        + [pltpu.SemaphoreType.DMA((kept, len(strips)))],
        input_output_aliases={5 + count + i: i for i in range(kept)} if so_far else {},
    )(scales, grad, *got, weight, *moments, *(so_far or ()), *deps)


def project(pieces, own, cot, so_far, last, deps, emit=()):
    tokens, width = own.shape
    kv = cot.shape[1]
    shard = width // lax.axis_size("fsdp")
    count = len(pieces)
    sizes = [piece[1] for piece in pieces]

    def kernel(*refs):
        weights, (cot_ref, own_ref) = refs[:count], refs[count : count + 2]
        at = count + 2
        if so_far:
            keys_ref = refs[at]
            at += 2
        at += len(deps)
        keys_out, back_out = refs[at : at + 2]
        spans_out = refs[at + 2 : at + 2 + len(emit)]
        at += 2 + len(emit)
        outs, shorts = refs[at : at + count], refs[at + count : at + count + len(emit)]
        keys_buf, sems = refs[-2:]
        stores = []
        for i, ((first, size), out) in enumerate(zip(emit, spans_out)):
            shorts[i][...] = weights[0][first : first + size, :].astype(BF16)
            stores.append(pltpu.make_async_copy(shorts[i], out, sems.at[count + 1 + i]))
            stores[-1].start()
        total = keys_ref[...] if so_far else None
        for j, (_, _, steps, other, first) in enumerate(pieces):
            place = pl.ds(pl.multiple_of(shard_at(steps, other) * shard + first, 128), sizes[j])
            rows = weights[j][: sizes[j], :].astype(BF16)
            outs[j][...] = lax.dot_general(
                cot_ref[...], rows, OVER_COLUMNS, preferred_element_type=F32
            ).astype(BF16)
            stores.append(pltpu.make_async_copy(outs[j], back_out.at[0, :, place], sems.at[j]))
            stores[-1].start()
            term = jnp.dot(own_ref[:, place], rows, preferred_element_type=F32)
            total = term if total is None else total + term
        if last:
            keys_buf[...] = total.astype(BF16)
            stores.append(pltpu.make_async_copy(keys_buf, keys_out.at[0], sems.at[count]))
            stores[-1].start()
        else:
            keys_out[...] = total
        for store in stores:
            store.wait()

    return call(
        kernel,
        "project",
        in_specs=[VMEM] * (count + 2) + ([VMEM, HBM] if so_far else []) + [ANY] * len(deps),
        out_specs=[HBM if last else VMEM, HBM] + [HBM] * len(emit),
        out_shape=[
            pltpu.HBM((1, tokens, kv), BF16) if last else like((tokens, kv), F32),
            pltpu.HBM((1, tokens, width), BF16),
        ]
        + [pltpu.HBM((size, kv), BF16) for _, size in emit],
        scratch_shapes=[pltpu.VMEM((tokens, size), BF16) for size in sizes]
        + [pltpu.VMEM((size, kv), BF16) for _, size in emit]
        + [pltpu.VMEM((tokens, kv), BF16), pltpu.SemaphoreType.DMA((count + 1 + len(emit),))],
        input_output_aliases={count + 3: 1} if so_far else {},
    )(*[piece[0] for piece in pieces], cot, own, *(so_far or ()), *deps)


def average(rows, spans, updated, neighbours, so_far, deps):
    kv = updated[0].shape[1]
    count = len(spans)
    strips = [(j, first, *strip) for j, (first, size, _) in enumerate(spans) for strip in strips_of(size)]

    def kernel(*refs):
        out, buf, sems = refs[-3:]
        copies = []
        for i, (j, first, strip, high) in enumerate(strips):
            here = slice(strip, strip + high)
            at = pl.ds(first - spans[0][0] + strip, high)
            buf[at, :] = 0.5 * (refs[j][here, :] + refs[count + j][here, :].astype(F32))
            copies.append(
                pltpu.make_async_copy(buf.at[at, :], out.at[0, pl.ds(first + strip, high), :], sems.at[i])
            )
            copies[-1].start()
        for copy in copies:
            copy.wait()

    before = [] if so_far is None else [so_far]
    return call(
        kernel,
        "average",
        in_specs=[VMEM] * (2 * count) + [HBM] * len(before) + [ANY] * len(deps),
        out_specs=HBM,
        out_shape=pltpu.HBM((1, rows, kv), F32),
        scratch_shapes=[
            pltpu.VMEM((sum(size for _, size, _ in spans), kv), F32),
            pltpu.SemaphoreType.DMA((len(strips),)),
        ],
        input_output_aliases={2 * count: 0} if before else {},
    )(*updated, *neighbours, *before, *deps)


def make_branch(distance):
    def branch(hidden, key_grad, weight, moment1, moment2, step):
        chips = lax.axis_size("fsdp") // CORES
        own, cot, w = hidden[0], key_grad[0], weight[0]
        state_in = (w, moment1[0], moment2[0])
        rows = w.shape[0]
        far = range(1, chips)

        def local_pieces(w_sib):
            return [(held[0], rows, 0, False, 0), (w_sib, rows, 0, True, 0)]

        def send_far(part, i):
            return [chip_shift(part, s, f"far{i}") for s in far]

        def pieces_of(i, arrays, order):
            first, size = w_spans[i]
            return [(v, size, s, False, first) for v, s in zip(arrays, far)] + [
                (core_swap(after(v, *order), f"swap{i}"), size, s, True, first) for v, s in zip(arrays, far)
            ]

        def adam(i, state, deps):
            return adam_rows(
                g_spans[i], grad, [got[s][i] for s in far], held[0], held[1:], scales, state, bool(distance), deps
            )

        def partial(s, spans, dtype, deps):
            return partial_grad(own, sib, cot, cot_sib, -s % chips, spans, dtype, deps)

        if 2 * distance >= lax.axis_size("rep"):
            g_spans = spans_of(rows, (20, 19, 25))
            w_spans = [span[:2] for span in spans_of(rows, (3, 3, 2))]
            sib, cot_sib = core_swap(own, "hidden"), core_swap(cot, "cot")
            sent = {s: add_part(own_part(own, cot, -s % chips), sib, cot_sib, -s % chips, g_spans) for s in far}
            got = {s: [chip_shift(part, s, f"grad{i}") for i, part in enumerate(sent[s])] for s in far}
            w_sib = core_swap(after(w, *[sent[s][-1] for s in far]), "w_sib")
            grad, scales, *held = own_grad(own, sib, cot, cot_sib, state_in, step, [sent[s][-1] for s in far])
            keys, back, *parts = project(local_pieces(w_sib), own, cot, None, False, [grad], w_spans)
            there = [send_far(part, i) for i, part in enumerate(parts)]
            state, order, updated, ups, near = None, keys, None, [], []
            for i in range(len(g_spans)):
                if i > 1:
                    updated = order = average(rows, [g_spans[i - 2]], [ups[i - 2]], [near[i - 2]], updated, [order])
                *state, up, order = adam(i, state, [order])
                ups.append(up)
                near.append(rep_shift(order, distance, f"near{i}"))
            updated = average(rows, [g_spans[-2]], [ups[-2]], [near[-2]], updated, [order])
            pieces = [piece for i in range(len(there)) for piece in pieces_of(i, there[i], [updated])]
            keys, back = project(pieces, own, cot, (keys, back), True, [updated])
            updated = average(rows, [g_spans[-1]], [ups[-1]], [near[-1]], updated, [keys])
        elif distance:
            g_spans = spans_of(rows, (25, 20, 19))
            w_spans = [span[:2] for span in spans_of(rows, (2, 3, 3))]
            sent_spans = [(w_spans[i][0], w_spans[i][1] + pad) for i, pad in enumerate((PAD, PAD, 0))]
            sib, cot_sib = core_swap(own, "hidden"), core_swap(cot, "cot")
            (w0,) = cast_rows(w, sent_spans[:1], [])
            there = [send_far(w0, 0)]
            sent = {s: partial(s, g_spans, BF16, [w0]) for s in far}
            got = {s: [chip_shift(part, s, f"grad{i}") for i, part in enumerate(sent[s])] for s in far}
            w_sib = core_swap(after(w, w0), "w_sib")
            grad, scales, *held = own_grad(own, sib, cot, cot_sib, state_in, step, [sent[s][-1] for s in far])
            pieces = local_pieces(w_sib) + pieces_of(0, there[0], [grad])
            keys, back, *parts = project(pieces, own, cot, None, False, [grad], sent_spans[1:])
            there += [send_far(part, 1 + i) for i, part in enumerate(parts)]
            state, order, ups, near = None, keys, [], []
            for i in range(len(g_spans)):
                *state, up, order = adam(i, state, [order])
                ups.append(up)
                near.append(rep_shift(order, distance, f"near{i}"))
            here = len(far)
            pieces = pieces_of(1, there[1], [order])
            keys, back = project(pieces[:here], own, cot, (keys, back), False, [order])
            updated = average(rows, g_spans, ups, near, None, [keys])
            pieces = pieces[here:] + pieces_of(2, there[2], [updated])
            keys, back = project(pieces[:-here], own, cot, (keys, back), False, [updated])
            keys, back = project(pieces[-here:], own, cot, (keys, back), True, [])
        else:
            g_spans = spans_of(rows, (47, 17))
            w_spans = [span[:2] for span in spans_of(rows, (1, 1))]
            sib, w_sib = core_swap(own, "hidden"), core_swap(w, "w_sib")
            parts = cast_rows(w, w_spans, [])
            cot_sib = core_swap(after(cot, parts[0]), "cot")
            there = [send_far(part, i) for i, part in enumerate(parts)]
            sent = {s: partial(s, g_spans, BF16, [parts[0]]) for s in far}
            got = {s: [chip_shift(part, s, f"grad{i}") for i, part in enumerate(sent[s])] for s in far}
            grad, scales, *held = own_grad(own, sib, cot, cot_sib, state_in, step, [sent[s][-1] for s in far])
            keys, back = project(local_pieces(w_sib), own, cot, None, False, [grad])
            pieces = [piece for i in range(len(there)) for piece in pieces_of(i, there[i], [keys])]
            keys, back = project(pieces, own, cot, (keys, back), True, [keys])
            state = adam(0, None, [keys])
            state = adam(1, state, [])
            updated = state[2]
        return keys, back, updated, state[0], state[1]

    return branch


def per_device(hidden, key_grad, weight, moment1, moment2, step):
    replicas = lax.axis_size("rep")
    distances = [2**level % replicas for level in range(LEVELS)]
    kinds = sorted(set(distances))
    level = lax.rem(step, LEVELS)
    pick = jnp.int32(0)
    for i, d in enumerate(distances):
        pick = jnp.where(level == i, kinds.index(d), pick)
    return lax.switch(
        pick, [make_branch(d) for d in kinds], hidden, key_grad, weight, moment1, moment2, step
    )


def solution(mesh):
    spec = P("rep", "fsdp", None)
    return jax.shard_map(
        per_device,
        mesh=mesh,
        in_specs=(spec,) * 5 + (P(),),
        out_specs=(spec,) * 5,
        check_vma=False,
    )
```
